256 devices in a mesh: gy: 32 (over y, z), gz: 8 (over x, core).
Axes of the slice: x: 4, y: 4, z: 8, core: 2. Of those that a mesh axis runs over, the one named last changes fastest.
Arguments:
- grid_values: float32 [20, 256, 128, 256], P(None, 'gy', 'gz'), may hold values from -6 to 6
- spectral_weights: float32 [20, 20, 2, 32, 32, 16], P(None, None, None, 'gy', 'gz'), may hold values from -1.25 to 1.25
- bypass_weight: float32 [20, 20], replicated, may hold values from -1.25 to 1.25
- bias_vector: float32 [20], replicated, may hold values from -3 to 3
- cotangent: float32 [20, 256, 128, 256], P(None, 'gy', 'gz'), may hold values from -6 to 6
Outputs:
- output: float32 [20, 256, 128, 256], P(None, 'gy', 'gz')
- grad_values: float32 [20, 256, 128, 256], P(None, 'gy', 'gz')
- grad_weights: float32 [20, 20, 2, 32, 32, 16], P(None, None, None, 'gy', 'gz')
The draws below stay inside these ranges and needn't reach their ends.
All inputs are finite; a program needn't handle non-finite values.
Results may differ from the reference program's by a relative error of at most 0.00011.
Values sent between devices are 32-bit elements; how exact they have to be, the bound alone decides.
No kernel may reach another device: no remote copies, remote signals or barrier semaphores. Data moves between devices by JAX's collectives and lax.ppermute only.
A program may use at most 128 MiB of HBM per device.

```python
import math
import jax
import jax.numpy as jnp
from jax import lax

C = 20
NX = 256
NY = 256
NZ = 128
MODES = 16


def level_of(own_key, shape, split, least, high):
    level = 1.0
    for axis_at, parts in split:
        draws = jax.random.uniform(jax.random.fold_in(jax.random.fold_in(own_key, 6), axis_at), (parts,), jnp.float32, least / len(split), high / len(split))
        level = level * jnp.repeat(jnp.exp(draws), shape[axis_at] // parts).reshape((-1,) + (1,) * (len(shape) - 1 - axis_at))
    return level


def normal_values(key, shape, scale, reach, split=(), held_as=jnp.bfloat16):
    level = level_of(key, shape, split, -0.22, 0.18) if split else 1.0
    entries = jax.random.normal(key, shape, jnp.float32) * scale * level
    return jnp.minimum(jnp.maximum(entries, -reach), reach).astype(held_as)


def setup_inputs(seed: int = 0) -> dict:
    streams_of = jax.random.split(jax.random.key(seed), 6)
    grid_values = normal_values(streams_of[0], (C, NY, NZ, NX), 1.0, 6.0, ((1, 32), (2, 8)), jnp.float32)
    spectral_weights = normal_values(streams_of[1], (C, C, 2, 2 * MODES, 2 * MODES, MODES), C ** -0.5, 1.25, ((3, 32), (4, 8)), jnp.float32)
    bypass_weight = normal_values(streams_of[2], (C, C), C ** -0.5, 1.25, (), jnp.float32)
    bias_vector = normal_values(streams_of[3], (C,), 0.7, 3.0, (), jnp.float32)
    cotangent = normal_values(streams_of[4], (C, NY, NZ, NX), 1.0, 6.0, ((1, 32), (2, 8)), jnp.float32)
    return {"grid_values": grid_values, "spectral_weights": spectral_weights, "bypass_weight": bypass_weight, "bias_vector": bias_vector, "cotangent": cotangent}


highest = lax.Precision.HIGHEST

def contract(form, left, right):
    return jnp.einsum(form, left, right, precision=highest, preferred_element_type=jnp.float32)

def wave_table(length, count, both_signs):
    positions = jnp.arange(length, dtype=jnp.int32)
    frequency = jnp.arange(count, dtype=jnp.int32)
    if both_signs:
        frequency = jnp.where(frequency < count // 2, frequency, frequency - count)
    turns = positions[:, None] * frequency[None, :] % length
    angles = turns.astype(jnp.float32) * jnp.float32(2.0 * math.pi / length)
    return (jnp.cos(angles), jnp.sin(angles))

def depth_factor():
    depth = jnp.arange(MODES, dtype=jnp.int32)
    scale_each = 1.0 / (2.0 * math.sqrt(4.0 * MODES * MODES * MODES))
    return jnp.where(depth == 0, jnp.float32(1.0), jnp.float32(2.0)) * jnp.float32(scale_each)

def forward_modes(values):
    cos_wide, sin_wide = wave_table(NX, 2 * MODES, True)
    table_wide = jnp.concatenate([cos_wide, -sin_wide], 1)
    spread = contract('cyzx,xr->cyzr', values, table_wide)
    real_part = spread[..., :2 * MODES]
    imag_part = spread[..., 2 * MODES:]
    cos_lat, sin_lat = wave_table(NY, 2 * MODES, True)
    lat_real = contract('cyzk,yq->qczk', real_part, cos_lat) + contract('cyzk,yq->qczk', imag_part, sin_lat)
    lat_imag = contract('cyzk,yq->qczk', imag_part, cos_lat) - contract('cyzk,yq->qczk', real_part, sin_lat)
    cos_deep, sin_deep = wave_table(NZ, MODES, False)
    deep_real = contract('qczk,zp->qcpk', lat_real, cos_deep) + contract('qczk,zp->qcpk', lat_imag, sin_deep)
    deep_imag = contract('qczk,zp->qcpk', lat_imag, cos_deep) - contract('qczk,zp->qcpk', lat_real, sin_deep)
    return jnp.transpose(jnp.stack([deep_real, deep_imag], 3), (1, 3, 4, 0, 2))

def grid_field(mode_block):
    arranged = jnp.transpose(mode_block, (3, 0, 4, 1, 2))
    real_part = arranged[:, :, :, 0]
    imag_part = arranged[:, :, :, 1]
    cos_deep, sin_deep = wave_table(NZ, MODES, False)
    deep_real = contract('qcpk,zp->qczk', real_part, cos_deep) - contract('qcpk,zp->qczk', imag_part, sin_deep)
    deep_imag = contract('qcpk,zp->qczk', real_part, sin_deep) + contract('qcpk,zp->qczk', imag_part, cos_deep)
    cos_lat, sin_lat = wave_table(NY, 2 * MODES, True)
    lat_real = contract('qczk,yq->cyzk', deep_real, cos_lat) - contract('qczk,yq->cyzk', deep_imag, sin_lat)
    lat_imag = contract('qczk,yq->cyzk', deep_real, sin_lat) + contract('qczk,yq->cyzk', deep_imag, cos_lat)
    cos_wide, sin_wide = wave_table(NX, 2 * MODES, True)
    table_wide = jnp.concatenate([cos_wide.T, -sin_wide.T], 0)
    return contract('cyzr,rx->cyzx', jnp.concatenate([lat_real, lat_imag], 3), table_wide)

def combine_modes(mode_block, weights):
    real_part = mode_block[:, 0]
    imag_part = mode_block[:, 1]
    weight_real = weights[:, :, 0]
    weight_imag = weights[:, :, 1]
    out_real = contract('cxyz,cdxyz->dxyz', real_part, weight_real) - contract('cxyz,cdxyz->dxyz', imag_part, weight_imag)
    out_imag = contract('cxyz,cdxyz->dxyz', real_part, weight_imag) + contract('cxyz,cdxyz->dxyz', imag_part, weight_real)
    return jnp.stack([out_real, out_imag], 1)

def reference(grid_values, spectral_weights, bypass_weight, bias_vector, cotangent):
    scaling = jnp.float32(1.0 / math.sqrt(NX * NY * NZ))
    factor = depth_factor()

    def layer(values, weights, bypass, offsets):
        mode_block = forward_modes(values) * scaling
        mixed_modes = combine_modes(mode_block, weights) * factor
        before = grid_field(mixed_modes) + contract('cyzx,cd->dyzx', values, bypass) + offsets[:, None, None, None]
        return jax.nn.gelu(before)
    output, pullback = jax.vjp(layer, grid_values, spectral_weights, bypass_weight, bias_vector)
    grads = pullback(cotangent)
    return (output, grads[0], grads[1])
```

```python
import math

import numpy as np
import ml_dtypes

import jax
import jax.numpy as jnp
from jax import lax
from jax.experimental import pallas as pl
from jax.experimental.pallas import tpu as pltpu
from jax.sharding import PartitionSpec as P

C = 20
NX = 256
NY = 256
NZ = 128
MODES = 16
GY = 32
GZ = 8
YL = NY // GY
ZL = NZ // GZ
LANES = YL * ZL
REALS = 5
SLOT_ROWS = 104
WEIGHT_ROWS = 80
GRAD_ROWS = 8
KINDS = REALS * GZ

f32 = jnp.float32
bf16 = jnp.bfloat16
VMEM_LIMIT = 48 * 1024 * 1024


def slot_row(j, c):
    return j * C + c if j < 3 else 64 + (j - 3) * C + c


def halves(array):
    high = array.astype(np.float32).astype(ml_dtypes.bfloat16)
    low = (array - high.astype(np.float64)).astype(np.float32).astype(ml_dtypes.bfloat16)
    return high, low


def wide_table():
    x = np.arange(NX)
    table = np.zeros((REALS, GZ, NX))
    for p in range(GZ):
        for j, (freq, imag) in enumerate(
            ((2 * p, False), (2 * p, True), (None, False), (2 * p + 1, False), (2 * p + 1, True))
        ):
            if p == 0 and j == 1:
                freq, imag = 16, False
            if p == 0 and j == 2:
                freq, imag = 16, True
            if freq is None:
                continue
            angle = 2.0 * math.pi * ((x * freq) % NX) / NX
            table[j, p] = -np.sin(angle) if imag else np.cos(angle)
    return table.reshape(KINDS, NX)


def deep_table():
    z = np.arange(NZ)
    kz = np.arange(MODES)
    angle = 2.0 * math.pi * ((kz[:, None] * z[None, :]) % NZ) / NZ
    both = np.stack([np.cos(angle), -np.sin(angle)], 0).reshape(2, MODES, GZ, ZL)
    table = np.einsum("rkgz,yv->rkygvz", both, np.eye(YL))
    return table.reshape(2 * MODES * YL, GZ * LANES)


def lat_table():
    row = np.arange(2 * MODES)
    ky = 4 * (row % 8) + row // 8
    fy = np.where(ky < MODES, ky, ky - 2 * MODES)
    y = np.arange(NY)
    angle = 2.0 * math.pi * ((fy[:, None] * y[None, :]) % NY) / NY
    return np.concatenate([np.cos(angle), np.sin(angle)], 0)


def pair_select():
    select = np.zeros((2, 2, 2, 64, 2, 2, 32))

    def put(variant, mode, sign, real, imag):
        for c in range(C):
            r = real * C + c
            select[variant, 0, 0, r, mode, 0, c] += 1
            select[variant, 1, 1, r, mode, 0, c] += 1
            select[variant, 0, 1, r, mode, 1, c] += 1
            select[variant, 1, 0, r, mode, 1, c] -= 1
            if imag is not None:
                i = imag * C + c
                select[variant, 0, 1, i, mode, 0, c] -= sign
                select[variant, 1, 0, i, mode, 0, c] += sign
                select[variant, 0, 0, i, mode, 1, c] += sign
                select[variant, 1, 1, i, mode, 1, c] += sign

    put(0, 0, 1, 0, 1)
    put(0, 1, -1, 0, 1)
    put(1, 0, 1, 0, None)
    put(1, 1, -1, 1, 2)
    return select.reshape(2, 256, 128)


def split(value):
    high = value.astype(bf16)
    low = (value - high.astype(f32)).astype(bf16)
    return high, low


def dot(left, right, dims=((1,), (0,))):
    return lax.dot_general(left, right, (dims, ((), ())), preferred_element_type=f32)


def dot3(left, right, dims=((1,), (0,))):
    return (
        dot(left[0], right[0], dims) + dot(left[0], right[1], dims) + dot(left[1], right[0], dims)
    )


def dot_exact(value, table):
    high, low = split(value)
    rest = (value - high.astype(f32) - low.astype(f32)).astype(bf16)
    return dot(high, table) + dot(low, table) + dot(rest, table)


def lane_index(shape):
    return lax.broadcasted_iota(jnp.int32, shape, len(shape) - 1)


def turn(value, amount=64):
    return pltpu.roll(value, amount, 1)


def wide_forward(tables, values, out_ref, channel, stride):
    high, low = split(values)
    tall = dot(tables, high, ((1,), (1,)))
    part = tall[:KINDS] + tall[KINDS:] + dot(tables[:KINDS], low, ((1,), (1,)))
    for j in range(REALS):
        out_ref[pl.ds(slot_row(j, 0) + channel, GZ, stride=stride), :] = part[8 * j : 8 * j + 8]


def wide_inverse(coef_ref, table, channel, stride):
    rows = [
        coef_ref[pl.ds(slot_row(j, 0) + channel, GZ, stride=stride), :] for j in range(REALS)
    ]
    coef = jnp.concatenate(rows, 0)
    high = coef.astype(bf16).astype(f32)
    stacked = jnp.concatenate([high, high, coef - high, jnp.zeros((8, LANES), f32)], 0)
    return dot(stacked.T.astype(bf16), table)


def clear_rows(out_ref, stride):
    for row in range(3 * C, 64):
        out_ref[pl.ds(row, GZ, stride=stride), :] = jnp.zeros((GZ, LANES), f32)


STEP_C = 4


def first_kernel(tables_ref, values_ref, weights_ref, out_ref):
    step = pl.program_id(0)
    stride = SLOT_ROWS + WEIGHT_ROWS

    @pl.when(step == 0)
    def _():
        clear_rows(out_ref, stride)

    tables = tables_ref[...]
    for k in range(STEP_C):
        wide_forward(tables, values_ref[k], out_ref, step * STEP_C + k, stride)
    for pair in range(STEP_C // 2):
        for ky in range(4):
            for low in range(2):
                pieces = []
                for k in (2 * pair, 2 * pair + 1):
                    for part in range(2):
                        pieces.append(
                            weights_ref[k, part * 4 + ky, pl.ds(low, GZ, stride=2), :]
                        )
                        pieces.append(jnp.zeros((GZ, 32 - C), f32))
                row = SLOT_ROWS + low * 40 + (step * (STEP_C // 2) + pair) * 4 + ky
                out_ref[pl.ds(row, GZ, stride=stride), :] = jnp.concatenate(pieces, 1)


def first_call(values, weights, tables):
    rows = GZ * (SLOT_ROWS + WEIGHT_ROWS)
    return pl.pallas_call(
        first_kernel,
        grid=(C // STEP_C,),
        in_specs=[
            pl.BlockSpec((2 * KINDS, NX), lambda i: (0, 0)),
            pl.BlockSpec((STEP_C, LANES, NX), lambda i: (i, 0, 0)),
            pl.BlockSpec((STEP_C, 8, MODES, C), lambda i: (i, 0, 0, 0)),
        ],
        out_specs=pl.BlockSpec((rows, LANES), lambda i: (0, 0)),
        out_shape=jax.ShapeDtypeStruct((rows, LANES), f32),
        compiler_params=pltpu.CompilerParams(vmem_limit_bytes=VMEM_LIMIT),
    )(tables, values, weights)


def deep_forward(high, low, block_ref, out_ref):
    section = jnp.concatenate([block_ref[g, :SLOT_ROWS, :] for g in range(GZ)], 1)
    deep = dot3((high, low), split(section), ((1,), (1,)))
    deep = jnp.concatenate([deep, jnp.zeros((2 * LANES, 128 - SLOT_ROWS), f32)], 1)
    real = deep[:LANES]
    imag = deep[LANES:]
    left = lane_index(real.shape) < 64
    out_ref[:LANES, :] = jnp.where(left, real, turn(imag))
    out_ref[LANES:, :] = jnp.where(left, turn(real), imag)


def deep_kernel(high_ref, low_ref, block_ref, out_ref):
    deep_forward(high_ref[...], low_ref[...], block_ref, out_ref)


def deep_weights_kernel(place_ref, high_ref, low_ref, block_ref, out_ref, own_ref, other_ref):
    deep_forward(high_ref[...], low_ref[...], block_ref, out_ref)
    low = place_ref[0]
    first = pl.multiple_of(SLOT_ROWS + 40 * low, 8)
    second = pl.multiple_of(SLOT_ROWS + 40 - 40 * low, 8)
    own_ref[...] = block_ref[:, pl.ds(first, 40), :]
    other_ref[...] = block_ref[:, pl.ds(second, 40), :]


def vmem():
    return pl.BlockSpec(memory_space=pltpu.VMEM)


def smem():
    return pl.BlockSpec(memory_space=pltpu.SMEM)


def params():
    return pltpu.CompilerParams(vmem_limit_bytes=VMEM_LIMIT)


def deep_call(block, tables):
    return pl.pallas_call(
        deep_kernel,
        in_specs=[vmem()] * 3,
        out_specs=vmem(),
        out_shape=jax.ShapeDtypeStruct((2 * LANES, 128), f32),
        compiler_params=params(),
    )(*tables, block)


def deep_weights_call(place, block, tables):
    chunk = jax.ShapeDtypeStruct((GZ, 40, 128), f32)
    return pl.pallas_call(
        deep_weights_kernel,
        in_specs=[smem()] + [vmem()] * 3,
        out_specs=[vmem()] * 3,
        out_shape=[jax.ShapeDtypeStruct((2 * LANES, 128), f32), chunk, chunk],
        compiler_params=params(),
    )(place, *tables, block)


def lat_forward(lat, select, block):
    both = dot3(lat, split(block))
    wide = jnp.concatenate([both[:32], both[32:]], 1)
    return dot_exact(wide, select)


def lat_inverse(lat_back, select_back, modes):
    wide = dot_exact(modes, select_back)
    both = jnp.concatenate([wide[:, :128], wide[:, 128:]], 0)
    return dot3(lat_back, split(both))


def channel_weights(own_ref, other_ref, odd, pair):
    rows = [pl.ds(pair * 4 + ky, GZ, stride=40) for ky in range(4)]
    own = jnp.concatenate([own_ref[r, :] for r in rows], 0)
    other = jnp.concatenate([other_ref[r, :] for r in rows], 0)
    plus = jnp.where(odd, other, own)
    minus = jnp.where(odd, own, other)
    left = lane_index(plus.shape) < 64
    return jnp.where(left, plus, turn(minus)), jnp.where(left, turn(plus), minus)


def spread(modes, lane):
    left = lane_index(modes.shape) < 64
    return jnp.where(left, modes[:, lane : lane + 1], modes[:, 64 + lane : 65 + lane])


def swap_parts(value):
    real = lane_index(value.shape) % 64 < 32
    return jnp.where(real, turn(value, 96), turn(value, 32)), real


def mix_kernel(
    place_ref, level_ref, lat_h, lat_l, back_h, back_l, sel_ref, selb_ref, block_ref, own_ref,
    other_ref, out_ref, modes_ref
):
    odd = place_ref[1] == 1
    variant = place_ref[2]
    modes = lat_forward((lat_h[...], lat_l[...]), sel_ref[variant], block_ref[...])
    modes = modes * level_ref[0]
    modes_ref[...] = modes
    direct = jnp.zeros((32, 128), f32)
    crossed = jnp.zeros((32, 128), f32)
    for pair in range(C // 2):
        for k, weight in enumerate(channel_weights(own_ref, other_ref, odd, pair)):
            channel = 2 * pair + k
            direct = direct + spread(modes, channel) * weight
            crossed = crossed + spread(modes, 32 + channel) * weight
    swapped, real = swap_parts(crossed)
    mixed = (direct + jnp.where(real, -swapped, swapped)) * level_ref[1]
    out_ref[...] = lat_inverse((back_h[...], back_l[...]), selb_ref[variant], mixed)


def mix_call(place, level, lat, block, own, other):
    return pl.pallas_call(
        mix_kernel,
        in_specs=[smem(), smem()] + [vmem()] * 9,
        out_specs=[vmem()] * 2,
        out_shape=[
            jax.ShapeDtypeStruct((NY, 128), f32),
            jax.ShapeDtypeStruct((32, 128), f32),
        ],
        compiler_params=params(),
    )(place, level, *lat, block, own, other)


def adjoint_kernel(
    place_ref, level_ref, lat_h, lat_l, back_h, back_l, sel_ref, selb_ref, block_ref, own_ref,
    other_ref, modes_ref, out_ref, first_ref, second_ref
):
    odd = place_ref[1] == 1
    variant = place_ref[2]
    grad = lat_forward((lat_h[...], lat_l[...]), sel_ref[variant], block_ref[...])
    grad = grad * level_ref[1]
    modes = modes_ref[...]
    left = lane_index(grad.shape) < 64
    plus = jnp.where(left, modes, turn(grad))
    minus = jnp.where(left, turn(modes), grad)
    first_ref[...] = jnp.where(odd, minus, plus)
    second_ref[...] = jnp.where(odd, plus, minus)
    swapped, real = swap_parts(grad)
    crossed = jnp.where(real, swapped, -swapped)
    lane = lane_index(grad.shape)
    block = jnp.zeros((32, 128), f32)
    for pair in range(C // 2):
        for k, weight in enumerate(channel_weights(own_ref, other_ref, odd, pair)):
            channel = 2 * pair + k
            for part, term in enumerate((weight * grad, weight * crossed)):
                for mode in range(2):
                    total = jnp.sum(term[:, 64 * mode : 64 * mode + 64], axis=1, keepdims=True)
                    block = jnp.where(lane == 64 * mode + 32 * part + channel, total, block)
    block = block * level_ref[0]
    out_ref[...] = lat_inverse((back_h[...], back_l[...]), selb_ref[variant], block)


def adjoint_call(place, level, lat, block, own, other, modes):
    small = jax.ShapeDtypeStruct((32, 128), f32)
    return pl.pallas_call(
        adjoint_kernel,
        in_specs=[smem(), smem()] + [vmem()] * 10,
        out_specs=[vmem()] * 3,
        out_shape=[jax.ShapeDtypeStruct((NY, 128), f32), small, small],
        compiler_params=params(),
    )(place, level, *lat, block, own, other, modes)


def deep_inverse(high, low, block_ref, out_ref):
    first = block_ref[:LANES, :]
    second = block_ref[LANES:, :]
    left = lane_index(first.shape) < 64
    real = jnp.where(left, first, turn(second))
    imag = jnp.where(left, turn(first), second)
    flat = jnp.concatenate([real.T, imag.T], 1)
    section = dot3(split(flat), (high, low))
    for g in range(GZ):
        out_ref[g, :SLOT_ROWS, :] = section[:SLOT_ROWS, LANES * g : LANES * g + LANES]


def deep_inverse_kernel(high_ref, low_ref, block_ref, out_ref):
    deep_inverse(high_ref[...], low_ref[...], block_ref, out_ref)


def deep_inverse_grads_kernel(
    place_ref, high_ref, low_ref, block_ref, first_ref, second_ref, out_ref
):
    deep_inverse(high_ref[...], low_ref[...], block_ref, out_ref)
    minus = place_ref[0] == 1
    first = first_ref[...]
    second = second_ref[...]
    for low, rows in enumerate((jnp.where(minus, second, first), jnp.where(minus, first, second))):
        for ky in range(4):
            row = SLOT_ROWS + low * 4 + ky
            out_ref[:, row, :] = rows[8 * ky : 8 * ky + 8]


def deep_inverse_call(block, tables):
    return pl.pallas_call(
        deep_inverse_kernel,
        in_specs=[vmem()] * 3,
        out_specs=vmem(),
        out_shape=jax.ShapeDtypeStruct((GZ, SLOT_ROWS, 128), f32),
        compiler_params=params(),
    )(*tables, block)


def deep_inverse_grads_call(place, block, first, second, tables):
    return pl.pallas_call(
        deep_inverse_grads_kernel,
        in_specs=[smem()] + [vmem()] * 5,
        out_specs=vmem(),
        out_shape=jax.ShapeDtypeStruct((GZ, SLOT_ROWS + GRAD_ROWS, 128), f32),
        compiler_params=params(),
    )(place, *tables, block, first, second)


ROOT = math.sqrt(2.0 / math.pi)
CUBE = 0.044715


def bypass_product(bypass_ref, values):
    high, low = split(bypass_ref[...])
    value_high, value_low = split(values)
    tall = dot(jnp.concatenate([high, low], 0), value_high)
    return tall[: 8 * C] + tall[8 * C :] + dot(high, value_low)


def layer_kernel(
    tables_ref, back_ref, bypass_ref, bias_ref, coef_ref, values_ref, cot_ref, out_ref, slope_ref,
    send_ref, field, slopes
):
    step = pl.program_id(0)

    @pl.when(step == 0)
    def _():
        clear_rows(send_ref, SLOT_ROWS)
        for channel in range(C):
            field[channel] = wide_inverse(coef_ref, back_ref[...], channel, SLOT_ROWS)

    for half in range(2):
        rows = pl.ds(8 * half, 8)
        place = pl.ds(pl.multiple_of(step * ZL + 8 * half, 8), 8)
        values = values_ref[:, 0, rows, :].reshape(8 * C, NX)
        cot = cot_ref[:, 0, rows, :].reshape(8 * C, NX)
        before = (
            bypass_product(bypass_ref, values)
            + field[:, place, :].reshape(8 * C, NX)
            + bias_ref[...]
        )
        square = before * before
        bend = jnp.tanh(ROOT * before * (1.0 + CUBE * square))
        half_up = 0.5 + 0.5 * bend
        out = before * half_up
        rate = half_up + (0.5 * ROOT) * before * (1.0 - bend * bend) * (
            1.0 + (3.0 * CUBE) * square
        )
        slope = (cot * rate).reshape(C, 8, NX)
        out_ref[:, 0, rows, :] = out.reshape(C, 8, NX)
        slope_ref[:, 0, rows, :] = slope
        slopes[:, place, :] = slope

    @pl.when(step == YL - 1)
    def _():
        tables = tables_ref[...]
        for channel in range(C):
            wide_forward(tables, slopes[channel], send_ref, channel, SLOT_ROWS)


def whole(shape):
    return pl.BlockSpec(shape, lambda i: (0,) * len(shape))


def row_block():
    return pl.BlockSpec((C, 1, ZL, NX), lambda i: (0, i, 0, 0))


def layer_call(tables, back, bypass, bias, coef, values, cotangent):
    grid_shape = jax.ShapeDtypeStruct((C, YL, ZL, NX), f32)
    send_shape = (GZ * SLOT_ROWS, LANES)
    return pl.pallas_call(
        layer_kernel,
        grid=(YL,),
        in_specs=[
            whole(tables.shape),
            whole(back.shape),
            whole(bypass.shape),
            whole(bias.shape),
            whole(coef.shape),
            row_block(),
            row_block(),
        ],
        out_specs=[row_block(), row_block(), whole(send_shape)],
        out_shape=[grid_shape, grid_shape, jax.ShapeDtypeStruct(send_shape, f32)],
        scratch_shapes=[
            pltpu.VMEM((C, LANES, NX), f32),
            pltpu.VMEM((C, LANES, NX), f32),
        ],
        compiler_params=params(),
    )(tables, back, bypass, bias, coef, values, cotangent)


def last_kernel(back_ref, bypass_ref, coef_ref, slope_ref, out_ref, weight_ref, field, rows_ref):
    step = pl.program_id(0)
    stride = SLOT_ROWS + GRAD_ROWS

    @pl.when(step == 0)
    def _():
        for channel in range(C):
            field[channel] = wide_inverse(coef_ref, back_ref[...], channel, stride)
        for ky in range(4):
            for low in range(2):
                rows_ref[pl.ds(low, GZ, stride=2), :] = coef_ref[
                    pl.ds(SLOT_ROWS + 4 * low + ky, GZ, stride=stride), :
                ]
            pair = rows_ref[...]
            grad_real = turn(pair, 64)
            grad_imag = turn(pair, 32)
            for channel in range(C):
                real = pair[:, channel : channel + 1]
                imag = pair[:, 32 + channel : 33 + channel]
                weight_ref[channel, ky] = (real * grad_real + imag * grad_imag)[:, :C]
                weight_ref[channel, 4 + ky] = (real * grad_imag - imag * grad_real)[:, :C]

    for half in range(2):
        rows = pl.ds(8 * half, 8)
        place = pl.ds(pl.multiple_of(step * ZL + 8 * half, 8), 8)
        slope = slope_ref[:, 0, rows, :].reshape(8 * C, NX)
        total = bypass_product(bypass_ref, slope) + field[:, place, :].reshape(8 * C, NX)
        out_ref[:, 0, rows, :] = total.reshape(C, 8, NX)


def last_call(back, bypass, coef, slopes):
    weight_shape = (C, 8, MODES, C)
    return pl.pallas_call(
        last_kernel,
        grid=(YL,),
        in_specs=[whole(back.shape), whole(bypass.shape), whole(coef.shape), row_block()],
        out_specs=[row_block(), whole(weight_shape)],
        out_shape=[
            jax.ShapeDtypeStruct((C, YL, ZL, NX), f32),
            jax.ShapeDtypeStruct(weight_shape, f32),
        ],
        scratch_shapes=[pltpu.VMEM((C, LANES, NX), f32), pltpu.VMEM((MODES, 128), f32)],
        compiler_params=params(),
    )(back, bypass, coef, slopes)


def exchange(block, axis):
    return lax.all_to_all(block, axis, split_axis=0, concat_axis=0, tiled=True)


def weight_pairs(other):
    pairs = []
    for kx in range(2 * MODES):
        minus = kx >= MODES
        freq = 0 if kx == MODES else (kx if not minus else 2 * MODES - kx)
        for g in range(GZ):
            low = int(minus) if not other else 1 - int(minus)
            to_gy = 16 * (freq % 2) + 2 * g + low
            pairs.append((kx * GZ + g, to_gy * GZ + freq // 2))
    return pairs


def backward(pairs):
    return [(to, source) for source, to in pairs]


def shards(grid_values, spectral_weights, bypass_weight, bias_vector, cotangent):
    gy = lax.axis_index("gy")
    gz = lax.axis_index("gz")
    kz = gy % 16
    place = jnp.stack(
        [
            (gy >= MODES).astype(jnp.int32),
            (kz % 2).astype(jnp.int32),
            ((gz == 0) & (gy < 16)).astype(jnp.int32),
        ]
    )
    factor = jnp.where(kz == 0, f32(1.0), f32(2.0)) * f32(
        1.0 / (2.0 * math.sqrt(4.0 * MODES * MODES * MODES))
    )
    level = jnp.stack([f32(1.0 / math.sqrt(NX * NY * NZ)), factor])

    wide = wide_table()
    wide_high, wide_low = halves(wide)
    tables = jnp.asarray(np.concatenate([wide_high, wide_low], 0))
    nothing = np.zeros((8, NX), ml_dtypes.bfloat16)
    back = jnp.asarray(np.concatenate([wide_high, wide_low, wide_high, nothing], 0))
    deep = tuple(jnp.asarray(t) for t in halves(deep_table()))
    lat = lat_table()
    select = pair_select()
    lat_tables = (
        *(jnp.asarray(t) for t in halves(lat)),
        *(jnp.asarray(t) for t in halves(lat.T.copy())),
        jnp.asarray(select.astype(ml_dtypes.bfloat16)),
        jnp.asarray(select.transpose(0, 2, 1).copy().astype(ml_dtypes.bfloat16)),
    )
    eye = jnp.eye(8, dtype=f32)
    bypass_back = (bypass_weight[:, None, :, None] * eye[None, :, None, :]).reshape(8 * C, 8 * C)
    bypass = (bypass_weight.T[:, None, :, None] * eye[None, :, None, :]).reshape(8 * C, 8 * C)
    bias = jnp.repeat(bias_vector, 8)[:, None]

    weights = jnp.transpose(spectral_weights, (0, 2, 3, 4, 5, 1)).reshape(C, 8, MODES, C)
    values = grid_values.reshape(C, LANES, NX)

    sent = first_call(values, weights, tables).reshape(GZ, SLOT_ROWS + WEIGHT_ROWS, LANES)
    got = exchange(sent, "gz")
    rows, own, other = deep_weights_call(place, got, deep)
    axes = ("gy", "gz")
    to_own = weight_pairs(False)
    to_other = weight_pairs(True)
    own = lax.ppermute(own, axes, to_own).reshape(GZ * 40, 128)
    other = lax.ppermute(other, axes, to_other).reshape(GZ * 40, 128)
    got = exchange(rows.reshape(GY, YL, 128), "gy").reshape(NY, 128)
    rows, modes = mix_call(place, level, lat_tables, got, own, other)
    got = exchange(rows.reshape(GY, YL, 128), "gy").reshape(2 * LANES, 128)
    got = exchange(deep_inverse_call(got, deep), "gz").reshape(GZ * SLOT_ROWS, LANES)
    output, slopes, sent = layer_call(tables, back, bypass, bias, got, grid_values, cotangent)

    got = exchange(sent.reshape(GZ, SLOT_ROWS, LANES), "gz")
    rows = deep_call(got, deep)
    got = exchange(rows.reshape(GY, YL, 128), "gy").reshape(NY, 128)
    rows, first, second = adjoint_call(place, level, lat_tables, got, own, other, modes)
    first = lax.ppermute(first, axes, backward(to_own))
    second = lax.ppermute(second, axes, backward(to_other))
    got = exchange(rows.reshape(GY, YL, 128), "gy").reshape(2 * LANES, 128)
    got = exchange(deep_inverse_grads_call(place, got, first, second, deep), "gz")
    got = got.reshape(GZ * (SLOT_ROWS + GRAD_ROWS), LANES)
    grad_values, weight_grad = last_call(back, bypass_back, got, slopes)
    weight_grad = weight_grad.reshape(C, 2, 1, 4, MODES, C)
    return output, grad_values, jnp.transpose(weight_grad, (0, 5, 1, 2, 3, 4))


def solution(mesh):
    in_specs = (
        P(None, "gy", "gz", None),
        P(None, None, None, "gy", "gz", None),
        P(),
        P(),
        P(None, "gy", "gz", None),
    )
    out_specs = (
        P(None, "gy", "gz", None),
        P(None, "gy", "gz", None),
        P(None, None, None, "gy", "gz", None),
    )
    return jax.shard_map(shards, mesh=mesh, in_specs=in_specs, out_specs=out_specs, check_vma=False)
```

```python
import math

import numpy as np
import ml_dtypes

import jax
import jax.numpy as jnp
from jax import lax
from jax.experimental import pallas as pl
from jax.experimental.pallas import tpu as pltpu
from jax.sharding import PartitionSpec as P

C = 20
NX = 256
NY = 256
NZ = 128
MODES = 16
GY = 32
GZ = 8
YL = NY // GY
ZL = NZ // GZ
LANES = YL * ZL
TILES = 5
SEND_ROWS = TILES * 32
WEIGHT_ROWS = 56
GRAD_ROWS = 8
EXTRA = 748
COEF_ROWS = 768
KINDS = 40

f32 = jnp.float32
bf16 = jnp.bfloat16
VMEM_LIMIT = 8 * 1024 * 1024
WIDE_LIMIT = 16 * 1024 * 1024
FIRST_LIMIT = 62200000
DEEP_ROWS = 2 * 2 * LANES
TABLE_ROWS = DEEP_ROWS + 2 * KINDS

GROUPS = (0, 160, 320, 480)


def halves(array):
    high = array.astype(np.float32).astype(ml_dtypes.bfloat16)
    low = (array - high.astype(np.float64)).astype(np.float32).astype(ml_dtypes.bfloat16)
    return high, low


def wide_table():
    x = np.arange(NX)
    freq = np.concatenate([np.arange(16), np.arange(1, 17), [16]])
    angle = 2.0 * math.pi * ((freq[:, None] * x[None, :]) % NX) / NX
    table = np.zeros((KINDS, NX))
    table[:33] = np.cos(angle)
    table[16:32] = -np.sin(angle[16:32])
    return table


def deep_table():
    z = np.arange(NZ)
    kz = np.arange(MODES)
    angle = 2.0 * math.pi * ((kz[:, None] * z[None, :]) % NZ) / NZ
    cos, sin = np.cos(angle), np.sin(angle)
    both = np.stack([np.stack([cos, -sin], 1), np.stack([sin, cos], 1)], 0)
    both = both.reshape(2, MODES, 2, GZ, ZL)
    table = np.einsum("akrgz,yv->gakryvz", both, np.eye(YL))
    return table.reshape(GZ, 2, 2 * MODES * YL, LANES)


def lat_table():
    row = np.arange(2 * MODES)
    ky = 4 * (row % 8) + row // 8
    fy = np.where(ky < MODES, ky, ky - 2 * MODES)
    y = np.arange(NY)
    angle = 2.0 * math.pi * ((fy[:, None] * y[None, :]) % NY) / NY
    return np.concatenate([np.cos(angle), np.sin(angle)], 0)


def split(value):
    high = value.astype(bf16)
    low = (value - high.astype(f32)).astype(bf16)
    return high, low


def dot(left, right, dims=((1,), (0,))):
    return lax.dot_general(left, right, (dims, ((), ())), preferred_element_type=f32)


def dot3(left, right, dims=((1,), (0,))):
    return (
        dot(left[0], right[0], dims) + dot(left[0], right[1], dims) + dot(left[1], right[0], dims)
    )


def lane_index(shape):
    return lax.broadcasted_iota(jnp.int32, shape, len(shape) - 1)


def turn(value, amount):
    amount = amount % 128
    return value if amount == 0 else pltpu.roll(value, amount, 1)


def times_i(value):
    lane = lane_index(value.shape) % 64
    turned = jnp.where(lane < C, -turn(value, -C), turn(value, C))
    return jnp.where(lane < 2 * C, turned, 0.0)


def wide_forward(tables, values, coef_ref, channel):
    high, low = split(values)
    tall = dot(tables, high, ((1,), (1,)))
    part = tall[:KINDS] + tall[KINDS:] + dot(tables[:KINDS], low, ((1,), (1,)))
    for k, start in enumerate(GROUPS):
        coef_ref[pl.ds(start + channel, 8, stride=C), :] = part[8 * k : 8 * k + 8]
    coef_ref[pl.ds(EXTRA + channel, 1), :] = part[32:33]


def wide_inverse(coef_ref, table, channel):
    rows = [coef_ref[pl.ds(start + channel, 8, stride=C), :] for start in GROUPS]
    rows.append(coef_ref[pl.ds(EXTRA + channel, 1), :])
    rows.append(jnp.zeros((7, LANES), f32))
    coef = jnp.concatenate(rows, 0)
    high = coef.astype(bf16).astype(f32)
    stacked = jnp.concatenate([high, high, coef - high, jnp.zeros((8, LANES), f32)], 0)
    return dot(stacked.T.astype(bf16), table)


def clear_extra(coef_ref):
    coef_ref[640:EXTRA, :] = jnp.zeros((EXTRA - 640, LANES), f32)


def deep_forward(deep_ref, coef_ref, out_ref):
    def product(at, rows):
        high, low = split(rows)
        table = deep_ref[2 * LANES * at : 2 * LANES * at + 2 * LANES, :]
        return dot(table, jnp.concatenate([high, high, low], 1), ((1,), (1,)))

    real = product(0, jnp.concatenate([coef_ref[0:384, :], coef_ref[640:COEF_ROWS, :]], 0))
    imag = product(1, coef_ref[256:640, :])
    left = lane_index((2 * LANES, 128)) < 64
    tiles = (
        real[:, :128],
        real[:, 128:256],
        jnp.where(left, real[:, 256:384], imag[:, :128]),
        imag[:, 128:256],
        imag[:, 256:] - real[:, 384:],
    )
    for t, deep in enumerate(tiles):
        for g in range(GZ):
            out_ref[g, 32 * t : 32 * t + 32, :] = deep[32 * g : 32 * g + 32]


def deep_inverse(deep_ref, block_ref, coef_ref):
    def product(at, rows):
        high, low = split(rows)
        table = deep_ref[2 * LANES * at : 2 * LANES * at + 2 * LANES, : 2 * LANES]
        wide = dot(high, table)
        return wide[:, :LANES] + wide[:, LANES:] + dot(low, table[:, :LANES])

    sections = []
    for t in range(TILES):
        tile = jnp.concatenate([block_ref[g, 32 * t : 32 * t + 32, :] for g in range(GZ)], 0)
        sections.append(tile.T)
    rows = jnp.concatenate(sections, 0)
    real = product(0, jnp.concatenate([rows[:320], -rows[512:]], 0))
    coef_ref[0:320, :] = real[:320]
    coef_ref[640:COEF_ROWS, :] = real[320:]
    coef_ref[320:640, :] = product(1, rows[320:])


STEP_C = 4
STEPS = C // STEP_C


class Fetch:
    def __init__(self, sems):
        self.sems = sems
        self.count = 0

    def start(self, source, target):
        copy = pltpu.make_async_copy(source, target, self.sems.at[self.count])
        self.count += 1
        copy.start()
        return copy


def fetch_deep(fetch, deep_hbm, deep):
    return fetch.start(deep_hbm.at[lax.axis_index("gz")], deep)


def pack_weights(weights_ref, out_ref):
    units = []
    for c in range(C):
        for ky in range(4):
            for low in range(2):
                for part in range(2):
                    units.append(weights_ref[c, part * 4 + ky, pl.ds(low, GZ, stride=2), :])
    for row in range(WEIGHT_ROWS):
        pieces = units[6 * row : 6 * row + 6]
        used = C * len(pieces)
        pieces.append(jnp.zeros((GZ, 128 - used), f32))
        out_ref[:, SEND_ROWS + row, :] = jnp.concatenate(pieces, 1)


def first_kernel(
    deep_hbm, values_hbm, weights_hbm, out_ref, deep, values, weights, coef, sems
):
    fetch = Fetch(sems)
    deep_copy = fetch_deep(fetch, deep_hbm, deep)
    copies = []
    for k in range(STEPS):
        part = pl.ds(k * STEP_C, STEP_C)
        copies.append(fetch.start(values_hbm.at[part], values.at[part]))
    weights_copy = fetch.start(weights_hbm, weights)
    clear_extra(coef)
    deep_copy.wait()
    for k in range(STEPS):
        copies[k].wait()
        for channel in range(k * STEP_C, k * STEP_C + STEP_C):
            wide_forward(deep[DEEP_ROWS:, :NX], values[channel], coef, channel)
    weights_copy.wait()
    pack_weights(weights, out_ref)
    deep_forward(deep, coef, out_ref)


def anywhere():
    return pl.BlockSpec(memory_space=pl.ANY)


def vmem():
    return pl.BlockSpec(memory_space=pltpu.VMEM)


def params(limit=VMEM_LIMIT):
    return pltpu.CompilerParams(vmem_limit_bytes=limit)


def deep_scratch():
    return pltpu.VMEM((TABLE_ROWS, 3 * LANES), bf16)


def first_call(deep, values, weights):
    shape = (GZ, SEND_ROWS + WEIGHT_ROWS, 128)
    return pl.pallas_call(
        first_kernel,
        in_specs=[anywhere()] * 3,
        out_specs=vmem(),
        out_shape=jax.ShapeDtypeStruct(shape, f32),
        scratch_shapes=[
            deep_scratch(),
            pltpu.VMEM(values.shape, f32),
            pltpu.VMEM(weights.shape, f32),
            pltpu.VMEM((COEF_ROWS, LANES), f32),
            pltpu.SemaphoreType.DMA((STEPS + 2,)),
        ],
        compiler_params=params(FIRST_LIMIT),
    )(deep, values, weights)


def join_kernel(block_ref, out_ref):
    tiles = []
    for t in range(TILES):
        rows = slice(32 * t, 32 * t + 32)
        total = block_ref[0, rows, :]
        for g in range(1, GZ):
            total = total + block_ref[g, rows, :]
        tiles.append(total)
    joined = jnp.concatenate(tiles, 1)
    gap = jnp.zeros((YL, 64 - 2 * C), f32)

    def arranged(at):
        cut = joined[:, C * at : C * at + C]
        return jnp.concatenate([cut[0:8], cut[8:16], gap, cut[16:24], cut[24:32], gap], 1)

    out_ref[0:8, :] = arranged(0)
    for f in range(1, 16):
        real = arranged(f)
        imag = arranged(15 + f)
        out_ref[8 * f : 8 * f + 8, :] = real + imag
        out_ref[8 * (32 - f) : 8 * (32 - f) + 8, :] = real - imag
    out_ref[128:136, :] = -arranged(31)


def join_call(block):
    return pl.pallas_call(
        join_kernel,
        in_specs=[vmem()],
        out_specs=vmem(),
        out_shape=jax.ShapeDtypeStruct((NY, 128), f32),
        compiler_params=params(),
    )(block)


def fork_blocks(block_ref, out_ref):
    blocks = [block_ref[0:8, :]]
    differences = []
    for f in range(1, 16):
        plus = block_ref[8 * f : 8 * f + 8, :]
        minus = block_ref[8 * (32 - f) : 8 * (32 - f) + 8, :]
        blocks.append(plus + minus)
        differences.append(plus - minus)
    blocks = blocks + differences + [-block_ref[128:136, :]]
    for k in range(4):
        lane = 64 * (k // 2) + C * (k % 2)
        row = jnp.concatenate([b[:, lane : lane + C] for b in blocks], 1)
        for t in range(TILES):
            piece = row[:, 128 * t : 128 * t + 128]
            for g in range(GZ):
                out_ref[g, 32 * t + 8 * k : 32 * t + 8 * k + 8, :] = piece


def fork_kernel(block_ref, out_ref):
    fork_blocks(block_ref, out_ref)


def fork_grads_kernel(block_ref, modes_ref, grad_ref, out_ref):
    fork_blocks(block_ref, out_ref)
    for ky in range(4):
        out_ref[:, SEND_ROWS + ky, :] = modes_ref[8 * ky : 8 * ky + 8, :]
        out_ref[:, SEND_ROWS + 4 + ky, :] = grad_ref[8 * ky : 8 * ky + 8, :]


def fork_call(block, *grads):
    rows = SEND_ROWS + (GRAD_ROWS if grads else 0)
    return pl.pallas_call(
        fork_grads_kernel if grads else fork_kernel,
        in_specs=[vmem()] * (1 + len(grads)),
        out_specs=vmem(),
        out_shape=jax.ShapeDtypeStruct((GZ, rows, 128), f32),
        compiler_params=params(),
    )(block, *grads)


def unpack(block_ref, c):
    left = lane_index((GZ, 128)) < 64
    rows = []
    for ky in range(4):
        sides = []
        for low in range(2):
            unit = (c * 4 + ky) * 2 + low
            side = block_ref[:, SEND_ROWS + unit // 3, :]
            sides.append(turn(side, 64 * low - 40 * (unit % 3)))
        rows.append(jnp.where(left, sides[0], sides[1]))
    return jnp.concatenate(rows, 0)


def lat_forward(lat, block):
    both = dot3(lat, split(block))
    return both[:32] - times_i(both[32:])


def lat_inverse(lat_back, modes):
    return dot3(lat_back, split(jnp.concatenate([modes, times_i(modes)], 0)))


def spread(modes, lane):
    left = lane_index(modes.shape) < 64
    return jnp.where(left, modes[:, lane : lane + 1], modes[:, 64 + lane : 65 + lane])


SCALING = 1.0 / math.sqrt(NX * NY * NZ)


def depth_factor():
    lane = lane_index((32, 128))
    first = (lane < 64) & (lax.axis_index("gz") == 0)
    scale = 1.0 / (2.0 * math.sqrt(4.0 * MODES * MODES * MODES))
    factor = jnp.where(first, f32(scale), f32(2.0 * scale))
    return jnp.where(lane % 64 < 2 * C, factor, 0.0)


def mix_kernel(
    lat_h, lat_l, back_h, back_l, block_ref, first_ref, out_ref, modes_ref, weights_ref
):
    modes = lat_forward((lat_h[...], lat_l[...]), block_ref[...]) * SCALING
    modes_ref[...] = modes
    direct = jnp.zeros((32, 128), f32)
    crossed = jnp.zeros((32, 128), f32)
    for c in range(C):
        weight = unpack(first_ref, c)
        weights_ref[c] = weight
        direct = direct + spread(modes, c) * weight
        crossed = crossed + spread(modes, C + c) * weight
    mixed = (direct + times_i(crossed)) * depth_factor()
    out_ref[...] = lat_inverse((back_h[...], back_l[...]), mixed)


def mix_call(lat, block, first):
    return pl.pallas_call(
        mix_kernel,
        in_specs=[vmem()] * 6,
        out_specs=[vmem()] * 3,
        out_shape=[
            jax.ShapeDtypeStruct((NY, 128), f32),
            jax.ShapeDtypeStruct((32, 128), f32),
            jax.ShapeDtypeStruct((C, 32, 128), f32),
        ],
        compiler_params=params(),
    )(*lat, block, first)


def join_table():
    table = np.zeros((C, 2, 128, 128))
    for c in range(C):
        for part in range(2):
            for low in range(2):
                table[c, part, 64 * low : 64 * low + 2 * C, 64 * low + C * part + c] = 1
    return table.reshape(2 * 128 * C, 128)


def adjoint_kernel(
    lat_h, lat_l, back_h, back_l, join_ref, block_ref, weights_ref, out_ref, grad_ref
):
    grad = lat_forward((lat_h[...], lat_l[...]), block_ref[...]) * depth_factor()
    grad_ref[...] = grad
    crossed = -times_i(grad)
    terms = []
    for c in range(C):
        weight = weights_ref[c]
        terms += [weight * grad, weight * crossed]
    high, low = split(jnp.concatenate(terms, 1))
    both = dot(jnp.concatenate([high, low], 0), join_ref[...])
    block = both[:32] + both[32:]
    out_ref[...] = lat_inverse((back_h[...], back_l[...]), block * SCALING)


def adjoint_call(lat, joins, block, weights):
    return pl.pallas_call(
        adjoint_kernel,
        in_specs=[vmem()] * 7,
        out_specs=[vmem()] * 2,
        out_shape=[
            jax.ShapeDtypeStruct((NY, 128), f32),
            jax.ShapeDtypeStruct((32, 128), f32),
        ],
        compiler_params=params(),
    )(*lat, joins, block, weights)


ROOT = math.sqrt(2.0 / math.pi)
CUBE = 0.044715


def bypass_blocks(bypass, dims):
    row = lax.broadcasted_iota(jnp.int32, (8 * C, C), 0)
    column = lax.broadcasted_iota(jnp.int32, (8 * C, C), 1)
    select = (row // 8 == column).astype(f32).astype(bf16)
    row = lax.broadcasted_iota(jnp.int32, (8 * C, 8 * C), 0)
    column = lax.broadcasted_iota(jnp.int32, (8 * C, 8 * C), 1)
    same = row % 8 == column % 8
    blocks = []
    for half in split(bypass):
        wide = dot(dot(select, half, dims).astype(bf16), select, ((1,), (1,)))
        blocks.append(jnp.where(same, wide, 0.0))
    return jnp.concatenate(blocks, 0).astype(bf16)


def bypass_product(blocks, values):
    high, low = split(values)
    tall = dot(blocks, high)
    return tall[: 8 * C] + tall[8 * C :] + dot(blocks[: 8 * C], low)


def layer_kernel(
    back_ref, deep_hbm, bypass_hbm, bias_hbm, block_ref, values_hbm, cot_hbm,
    out_hbm, slope_hbm, send_ref, deep, bypass, bias, values, cots, field, coef, blocks,
    small_sems, value_sems, cot_sems, out_sems, slope_sems
):
    fetch = Fetch(small_sems)
    deep_copy = fetch_deep(fetch, deep_hbm, deep)
    bypass_copy = fetch.start(bypass_hbm, bypass)
    bias_copy = fetch.start(bias_hbm, bias)

    def value_copy(y):
        return pltpu.make_async_copy(values_hbm.at[:, y], values.at[:, y], value_sems.at[y])

    def cot_copy(y):
        return pltpu.make_async_copy(cot_hbm.at[:, y], cots.at[:, y], cot_sems.at[y])

    def out_copy(y):
        return pltpu.make_async_copy(values.at[:, y], out_hbm.at[:, y], out_sems.at[y])

    def slope_copy(y):
        return pltpu.make_async_copy(cots.at[:, y], slope_hbm.at[:, y], slope_sems.at[y])

    for y in range(YL):
        value_copy(y).start()
        cot_copy(y).start()
    deep_copy.wait()
    deep_inverse(deep, block_ref, coef)
    bypass_copy.wait()
    blocks[...] = bypass_blocks(bypass[...], ((1,), (1,)))
    bias_copy.wait()
    for channel in range(C):
        field[channel] = wide_inverse(coef, back_ref[...], channel) + bias[channel]

    @pl.loop(0, YL)
    def _(y):
        value_copy(y).wait()
        cot_copy(y).wait()
        for half in range(2):
            rows = pl.ds(8 * half, 8)
            place = pl.ds(pl.multiple_of(y * ZL + 8 * half, 8), 8)
            before = bypass_product(
                blocks[...], values[:, y, rows, :].reshape(8 * C, NX)
            ) + field[:, place, :].reshape(8 * C, NX)
            square = before * before
            bend = jnp.tanh(before * (ROOT + (ROOT * CUBE) * square))
            half_up = 0.5 + 0.5 * bend
            rate = half_up + (half_up - half_up * half_up) * before * (
                2.0 * ROOT + (6.0 * ROOT * CUBE) * square
            )
            cot = cots[:, y, rows, :].reshape(8 * C, NX)
            values[:, y, rows, :] = (before * half_up).reshape(C, 8, NX)
            cots[:, y, rows, :] = (cot * rate).reshape(C, 8, NX)
        out_copy(y).start()
        slope_copy(y).start()

    clear_extra(coef)
    for channel in range(C):
        wide_forward(deep[DEEP_ROWS:, :NX], cots[channel].reshape(LANES, NX), coef, channel)
    deep_forward(deep, coef, send_ref)
    for y in range(YL):
        out_copy(y).wait()
        slope_copy(y).wait()


def grid_buffer():
    return pltpu.VMEM((C, YL, ZL, NX), f32)


def layer_call(back, deep, bypass, bias, block, values, cotangent):
    grid_shape = jax.ShapeDtypeStruct((C, YL, ZL, NX), f32)
    many = pltpu.SemaphoreType.DMA((YL,))
    return pl.pallas_call(
        layer_kernel,
        in_specs=[vmem(), anywhere(), anywhere(), anywhere(), vmem()]
        + [anywhere()] * 2,
        out_specs=[anywhere(), anywhere(), vmem()],
        out_shape=[
            grid_shape,
            grid_shape,
            jax.ShapeDtypeStruct((GZ, SEND_ROWS, 128), f32),
        ],
        scratch_shapes=[
            deep_scratch(),
            pltpu.VMEM((C, C), f32),
            pltpu.SMEM((C,), f32),
            grid_buffer(),
            grid_buffer(),
            pltpu.VMEM((C, LANES, NX), f32),
            pltpu.VMEM((COEF_ROWS, LANES), f32),
            pltpu.VMEM((16 * C, 8 * C), bf16),
            pltpu.SemaphoreType.DMA((3,)),
            many,
            many,
            many,
            many,
        ],
        compiler_params=params(WIDE_LIMIT),
    )(back, deep, bypass, bias, block, values, cotangent)


def last_kernel(
    back_ref, deep_hbm, bypass_hbm, block_ref, slope_hbm, out_hbm, weight_hbm, deep, bypass,
    slopes, field, coef, blocks, weight, modes_rows, grad_rows, small_sems, slope_sems, out_sems
):
    fetch = Fetch(small_sems)
    deep_copy = fetch_deep(fetch, deep_hbm, deep)
    bypass_copy = fetch.start(bypass_hbm, bypass)

    def slope_copy(y):
        return pltpu.make_async_copy(slope_hbm.at[:, y], slopes.at[:, y], slope_sems.at[y])

    def out_copy(y):
        return pltpu.make_async_copy(slopes.at[:, y], out_hbm.at[:, y], out_sems.at[y])

    for y in range(YL):
        slope_copy(y).start()
    for ky in range(4):
        for low in range(2):
            rows = pl.ds(low, GZ, stride=2)
            modes_rows[rows, :] = turn(block_ref[:, SEND_ROWS + ky, :], 64 * low)
            grad_rows[rows, :] = turn(block_ref[:, SEND_ROWS + 4 + ky, :], 64 * low)
        modes = modes_rows[...]
        grad_real = grad_rows[...]
        grad_imag = turn(grad_real, -C)
        for channel in range(C):
            real = modes[:, channel : channel + 1]
            imag = modes[:, C + channel : C + channel + 1]
            weight[channel, ky] = (real * grad_real + imag * grad_imag)[:, :C]
            weight[channel, 4 + ky] = (real * grad_imag - imag * grad_real)[:, :C]
    weight_copy = fetch.start(weight, weight_hbm)
    deep_copy.wait()
    deep_inverse(deep, block_ref, coef)
    bypass_copy.wait()
    blocks[...] = bypass_blocks(bypass[...], ((1,), (0,)))
    for channel in range(C):
        field[channel] = wide_inverse(coef, back_ref[...], channel)

    @pl.loop(0, YL)
    def _(y):
        slope_copy(y).wait()
        for half in range(2):
            rows = pl.ds(8 * half, 8)
            place = pl.ds(pl.multiple_of(y * ZL + 8 * half, 8), 8)
            total = bypass_product(
                blocks[...], slopes[:, y, rows, :].reshape(8 * C, NX)
            ) + field[:, place, :].reshape(8 * C, NX)
            slopes[:, y, rows, :] = total.reshape(C, 8, NX)
        out_copy(y).start()

    for y in range(YL):
        out_copy(y).wait()
    weight_copy.wait()


def last_call(back, deep, bypass, block, slopes):
    weight_shape = (C, 8, MODES, C)
    many = pltpu.SemaphoreType.DMA((YL,))
    return pl.pallas_call(
        last_kernel,
        in_specs=[vmem(), anywhere(), anywhere(), vmem(), anywhere()],
        out_specs=[anywhere(), anywhere()],
        out_shape=[
            jax.ShapeDtypeStruct((C, YL, ZL, NX), f32),
            jax.ShapeDtypeStruct(weight_shape, f32),
        ],
        scratch_shapes=[
            deep_scratch(),
            pltpu.VMEM((C, C), f32),
            grid_buffer(),
            pltpu.VMEM((C, LANES, NX), f32),
            pltpu.VMEM((COEF_ROWS, LANES), f32),
            pltpu.VMEM((16 * C, 8 * C), bf16),
            pltpu.VMEM(weight_shape, f32),
            pltpu.VMEM((MODES, 128), f32),
            pltpu.VMEM((MODES, 128), f32),
            pltpu.SemaphoreType.DMA((3,)),
            many,
            many,
        ],
        compiler_params=params(WIDE_LIMIT),
    )(back, deep, bypass, block, slopes)


def exchange(block, axis):
    return lax.all_to_all(block, axis, split_axis=0, concat_axis=0, tiled=True)


def over_y(rows):
    return exchange(rows.reshape(GY, YL, 128), "gy").reshape(NY, 128)


def shards(grid_values, spectral_weights, bypass_weight, bias_vector, cotangent):
    wide_high, wide_low = halves(wide_table())
    nothing = np.zeros((8, NX), ml_dtypes.bfloat16)
    back = jnp.asarray(np.concatenate([wide_high, wide_low, wide_high, nothing], 0))
    deep_high, deep_low = halves(deep_table())
    deep = np.concatenate([deep_high, deep_low, deep_high], 3).reshape(GZ, DEEP_ROWS, 3 * LANES)
    wide = np.concatenate([wide_high, wide_low], 0)
    wide = np.concatenate([wide, np.zeros((2 * KINDS, LANES), ml_dtypes.bfloat16)], 1)
    deep = np.concatenate([deep, np.broadcast_to(wide, (GZ,) + wide.shape)], 1)
    deep = jnp.asarray(deep)
    joins = jnp.asarray(join_table().astype(ml_dtypes.bfloat16))
    lat_full = lat_table()
    lat = tuple(jnp.asarray(t) for t in halves(lat_full) + halves(lat_full.T.copy()))
    weights = jnp.transpose(spectral_weights, (0, 2, 3, 4, 5, 1)).reshape(C, 8, MODES, C)
    values = grid_values.reshape(C, LANES, NX)

    first = exchange(first_call(deep, values, weights), "gz")
    rows, modes, mixing = mix_call(lat, over_y(join_call(first)), first)
    got = exchange(fork_call(over_y(rows)), "gz")
    output, slopes, sent = layer_call(
        back, deep, bypass_weight, bias_vector, got, grid_values, cotangent
    )

    got = exchange(sent, "gz")
    rows, grad = adjoint_call(lat, joins, over_y(join_call(got)), mixing)
    got = exchange(fork_call(over_y(rows), modes, grad), "gz")
    grad_values, weight_grad = last_call(back, deep, bypass_weight, got, slopes)
    weight_grad = weight_grad.reshape(C, 2, 1, 4, MODES, C)
    return output, grad_values, jnp.transpose(weight_grad, (0, 5, 1, 2, 3, 4))


def solution(mesh):
    in_specs = (
        P(None, "gy", "gz", None),
        P(None, None, None, "gy", "gz", None),
        P(),
        P(),
        P(None, "gy", "gz", None),
    )
    out_specs = (
        P(None, "gy", "gz", None),
        P(None, "gy", "gz", None),
        P(None, None, None, "gy", "gz", None),
    )
    return jax.shard_map(shards, mesh=mesh, in_specs=in_specs, out_specs=out_specs, check_vma=False)
```

```python
import math

import numpy as np
import ml_dtypes

import jax
import jax.numpy as jnp
from jax import lax
from jax.experimental import pallas as pl
from jax.experimental.pallas import tpu as pltpu
from jax.sharding import PartitionSpec as P

C = 20
NX = 256
NY = 256
NZ = 128
MODES = 16
GY = 32
GZ = 8
YL = NY // GY
ZL = NZ // GZ
LANES = YL * ZL
TILES = 5
SEND_ROWS = TILES * 32
WEIGHT_ROWS = 56
GRAD_ROWS = 8
EXTRA = 748
COEF_ROWS = 768
KINDS = 40

f32 = jnp.float32
bf16 = jnp.bfloat16
VMEM_LIMIT = 8 * 1024 * 1024
WIDE_LIMIT = 20 * 1024 * 1024
DEEP_ROWS = 2 * 2 * LANES
TABLE_ROWS = DEEP_ROWS + NX

GROUPS = (0, 160, 320, 480)


def halves(array):
    high = array.astype(np.float32).astype(ml_dtypes.bfloat16)
    low = (array - high.astype(np.float64)).astype(np.float32).astype(ml_dtypes.bfloat16)
    return high, low


def wide_table():
    x = np.arange(NX)
    freq = np.concatenate([np.arange(16), np.arange(1, 17), [16]])
    angle = 2.0 * math.pi * ((freq[:, None] * x[None, :]) % NX) / NX
    table = np.zeros((KINDS, NX))
    table[:33] = np.cos(angle)
    table[16:32] = -np.sin(angle[16:32])
    return table


def deep_table():
    z = np.arange(NZ)
    kz = np.arange(MODES)
    angle = 2.0 * math.pi * ((kz[:, None] * z[None, :]) % NZ) / NZ
    cos, sin = np.cos(angle), np.sin(angle)
    both = np.stack([np.stack([cos, -sin], 1), np.stack([sin, cos], 1)], 0)
    both = both.reshape(2, MODES, 2, GZ, ZL)
    table = np.einsum("akrgz,yv->gakryvz", both, np.eye(YL))
    return table.reshape(GZ, 2, 2 * MODES * YL, LANES)


def lat_table():
    row = np.arange(2 * MODES)
    ky = 4 * (row % 8) + row // 8
    fy = np.where(ky < MODES, ky, ky - 2 * MODES)
    y = np.arange(NY)
    angle = 2.0 * math.pi * ((fy[:, None] * y[None, :]) % NY) / NY
    return np.concatenate([np.cos(angle), np.sin(angle)], 0)


def split(value):
    high = value.astype(bf16)
    low = (value - high.astype(f32)).astype(bf16)
    return high, low


def dot(left, right, dims=((1,), (0,))):
    return lax.dot_general(left, right, (dims, ((), ())), preferred_element_type=f32)


def dot3(left, right, dims=((1,), (0,))):
    return (
        dot(left[0], right[0], dims) + dot(left[0], right[1], dims) + dot(left[1], right[0], dims)
    )


def lane_index(shape):
    return lax.broadcasted_iota(jnp.int32, shape, len(shape) - 1)


def turn(value, amount):
    amount = amount % 128
    return value if amount == 0 else pltpu.roll(value, amount, 1)


def times_i(value):
    lane = lane_index(value.shape) % 64
    turned = jnp.where(lane < C, -turn(value, -C), turn(value, C))
    return jnp.where(lane < 2 * C, turned, 0.0)


PAIR = 2


def wide_forward(tables, values, coef_ref, channel):
    high, low = split(values)
    wide = dot(high, tables)
    part = wide[:, :LANES] + wide[:, LANES:] + dot(low, tables[:, :LANES])
    for n in range(values.shape[0] // LANES):
        rows = part[LANES * n : LANES * n + LANES].T
        for k, start in enumerate(GROUPS):
            coef_ref[pl.ds(start + channel + n, 8, stride=C), :] = rows[8 * k : 8 * k + 8]
        coef_ref[pl.ds(EXTRA + channel + n, 1), :] = rows[32:33]


def wide_inverse(coef_ref, table, channel):
    rows = [coef_ref[pl.ds(start + channel, 8, stride=C), :] for start in GROUPS]
    rows.append(coef_ref[pl.ds(EXTRA + channel, 1), :])
    rows.append(jnp.zeros((7, LANES), f32))
    coef = jnp.concatenate(rows, 0)
    high = coef.astype(bf16).astype(f32)
    stacked = jnp.concatenate([high, high, coef - high, jnp.zeros((8, LANES), f32)], 0)
    return dot(stacked.T.astype(bf16), table)


def clear_extra(coef_ref):
    coef_ref[640:EXTRA, :] = jnp.zeros((EXTRA - 640, LANES), f32)


def deep_forward(deep_ref, coef_ref, out_ref):
    def product(at, rows):
        high, low = split(rows)
        table = deep_ref[2 * LANES * at : 2 * LANES * at + 2 * LANES, :]
        return dot(table, jnp.concatenate([high, high, low], 1), ((1,), (1,)))

    real = product(0, jnp.concatenate([coef_ref[0:384, :], coef_ref[640:COEF_ROWS, :]], 0))
    imag = product(1, coef_ref[256:640, :])
    left = lane_index((2 * LANES, 128)) < 64
    tiles = (
        real[:, :128],
        real[:, 128:256],
        jnp.where(left, real[:, 256:384], imag[:, :128]),
        imag[:, 128:256],
        imag[:, 256:] - real[:, 384:],
    )
    for t, deep in enumerate(tiles):
        for g in range(GZ):
            out_ref[g, 32 * t : 32 * t + 32, :] = deep[32 * g : 32 * g + 32]


def deep_inverse(deep_ref, block_ref, coef_ref):
    def product(at, rows):
        high, low = split(rows)
        table = deep_ref[2 * LANES * at : 2 * LANES * at + 2 * LANES, : 2 * LANES]
        wide = dot(high, table)
        return wide[:, :LANES] + wide[:, LANES:] + dot(low, table[:, :LANES])

    sections = []
    for t in range(TILES):
        tile = jnp.concatenate([block_ref[g, 32 * t : 32 * t + 32, :] for g in range(GZ)], 0)
        sections.append(tile.T)
    rows = jnp.concatenate(sections, 0)
    real = product(0, jnp.concatenate([rows[:320], -rows[512:]], 0))
    coef_ref[0:320, :] = real[:320]
    coef_ref[640:COEF_ROWS, :] = real[320:]
    coef_ref[320:640, :] = product(1, rows[320:])


STEP_C = 4
STEPS = C // STEP_C


class Fetch:
    def __init__(self, sems):
        self.sems = sems
        self.count = 0

    def start(self, source, target):
        copy = pltpu.make_async_copy(source, target, self.sems.at[self.count])
        self.count += 1
        copy.start()
        return copy


def fetch_deep(fetch, deep_hbm, deep):
    return fetch.start(deep_hbm.at[lax.axis_index("gz")], deep)


def pack_weights(weights_ref, out_ref):
    units = []
    for c in range(C):
        for ky in range(4):
            for low in range(2):
                for part in range(2):
                    units.append(weights_ref[c, part * 4 + ky, pl.ds(low, GZ, stride=2), :])
    for row in range(WEIGHT_ROWS):
        pieces = units[6 * row : 6 * row + 6]
        used = C * len(pieces)
        pieces.append(jnp.zeros((GZ, 128 - used), f32))
        out_ref[:, SEND_ROWS + row, :] = jnp.concatenate(pieces, 1)


def first_kernel(
    deep_hbm, values_hbm, weights_hbm, out_ref, deep, values, weights, coef, sems
):
    fetch = Fetch(sems)
    deep_copy = fetch_deep(fetch, deep_hbm, deep)
    copies = []
    for k in range(STEPS):
        part = pl.ds(k * STEP_C, STEP_C)
        copies.append(fetch.start(values_hbm.at[part], values.at[part]))
    weights_copy = fetch.start(weights_hbm, weights)
    clear_extra(coef)
    deep_copy.wait()
    for k in range(STEPS):
        copies[k].wait()
        for channel in range(k * STEP_C, k * STEP_C + STEP_C, PAIR):
            both = values[channel : channel + PAIR].reshape(PAIR * LANES, NX)
            wide_forward(deep[DEEP_ROWS:, : 2 * LANES], both, coef, channel)
    weights_copy.wait()
    pack_weights(weights, out_ref)
    deep_forward(deep, coef, out_ref)


def anywhere():
    return pl.BlockSpec(memory_space=pl.ANY)


def vmem():
    return pl.BlockSpec(memory_space=pltpu.VMEM)


def params(limit=VMEM_LIMIT):
    return pltpu.CompilerParams(vmem_limit_bytes=limit)


def first_call(deep, values, weights):
    shape = (GZ, SEND_ROWS + WEIGHT_ROWS, 128)
    operands = (deep, values, weights)
    return pl.pallas_call(
        first_kernel,
        in_specs=[pl.BlockSpec(memory_space=pltpu.HBM)] * len(operands),
        out_specs=[vmem()] * 2,
        out_shape=[
            jax.ShapeDtypeStruct(shape, f32),
            jax.ShapeDtypeStruct((TABLE_ROWS, 3 * LANES), bf16),
        ],
        scratch_shapes=[
            pltpu.VMEM(values.shape, f32),
            pltpu.VMEM(weights.shape, f32),
            pltpu.VMEM((COEF_ROWS, LANES), f32),
            pltpu.SemaphoreType.DMA((STEPS + 3,)),
        ],
        compiler_params=params(WIDE_LIMIT),
    )(*(pltpu.with_memory_space_constraint(a, pltpu.HBM) for a in operands))


def join_kernel(block_ref, out_ref):
    tiles = []
    for t in range(TILES):
        rows = slice(32 * t, 32 * t + 32)
        total = block_ref[0, rows, :]
        for g in range(1, GZ):
            total = total + block_ref[g, rows, :]
        tiles.append(total)
    joined = jnp.concatenate(tiles, 1)
    gap = jnp.zeros((YL, 64 - 2 * C), f32)

    def arranged(at):
        cut = joined[:, C * at : C * at + C]
        return jnp.concatenate([cut[0:8], cut[8:16], gap, cut[16:24], cut[24:32], gap], 1)

    out_ref[0:8, :] = arranged(0)
    for f in range(1, 16):
        real = arranged(f)
        imag = arranged(15 + f)
        out_ref[8 * f : 8 * f + 8, :] = real + imag
        out_ref[8 * (32 - f) : 8 * (32 - f) + 8, :] = real - imag
    out_ref[128:136, :] = -arranged(31)


def join_call(block):
    return pl.pallas_call(
        join_kernel,
        in_specs=[vmem()],
        out_specs=vmem(),
        out_shape=jax.ShapeDtypeStruct((NY, 128), f32),
        compiler_params=params(),
    )(block)


def fork_blocks(block_ref, out_ref, copies):
    blocks = [block_ref[0:8, :]]
    differences = []
    for f in range(1, 16):
        plus = block_ref[8 * f : 8 * f + 8, :]
        minus = block_ref[8 * (32 - f) : 8 * (32 - f) + 8, :]
        blocks.append(plus + minus)
        differences.append(plus - minus)
    blocks = blocks + differences + [-block_ref[128:136, :]]
    for k in range(4):
        lane = 64 * (k // 2) + C * (k % 2)
        row = jnp.concatenate([b[:, lane : lane + C] for b in blocks], 1)
        for t in range(TILES):
            piece = row[:, 128 * t : 128 * t + 128]
            for g in range(copies):
                out_ref[g, 32 * t + 8 * k : 32 * t + 8 * k + 8, :] = piece


def fork_kernel(block_ref, out_ref):
    fork_blocks(block_ref, out_ref, 1)


def fork_grads_kernel(block_ref, modes_ref, grad_ref, out_ref):
    fork_blocks(block_ref, out_ref, GZ)
    for ky in range(4):
        out_ref[:, SEND_ROWS + ky, :] = modes_ref[8 * ky : 8 * ky + 8, :]
        out_ref[:, SEND_ROWS + 4 + ky, :] = grad_ref[8 * ky : 8 * ky + 8, :]


def fork_call(block, *grads):
    rows = SEND_ROWS + (GRAD_ROWS if grads else 0)
    return pl.pallas_call(
        fork_grads_kernel if grads else fork_kernel,
        in_specs=[vmem()] * (1 + len(grads)),
        out_specs=vmem(),
        out_shape=jax.ShapeDtypeStruct((GZ if grads else 1, rows, 128), f32),
        compiler_params=params(),
    )(block, *grads)


def unpack(block_ref, c):
    left = lane_index((GZ, 128)) < 64
    rows = []
    for ky in range(4):
        sides = []
        for low in range(2):
            unit = (c * 4 + ky) * 2 + low
            side = block_ref[:, SEND_ROWS + unit // 3, :]
            sides.append(turn(side, 64 * low - 40 * (unit % 3)))
        rows.append(jnp.where(left, sides[0], sides[1]))
    return jnp.concatenate(rows, 0)


def lat_forward(lat, block):
    both = dot3(lat, split(block))
    return both[:32] - times_i(both[32:])


def lat_inverse(lat_back, modes):
    return dot3(lat_back, split(jnp.concatenate([modes, times_i(modes)], 0)))


def spread(modes, lane):
    left = lane_index(modes.shape) < 64
    return jnp.where(left, modes[:, lane : lane + 1], modes[:, 64 + lane : 65 + lane])


SCALING = 1.0 / math.sqrt(NX * NY * NZ)


def depth_factor():
    lane = lane_index((32, 128))
    first = (lane < 64) & (lax.axis_index("gz") == 0)
    scale = 1.0 / (2.0 * math.sqrt(4.0 * MODES * MODES * MODES))
    factor = jnp.where(first, f32(scale), f32(2.0 * scale))
    return jnp.where(lane % 64 < 2 * C, factor, 0.0)


def mix_kernel(
    lat_h, lat_l, back_h, back_l, block_ref, first_ref, out_ref, modes_ref, weights_ref
):
    modes = lat_forward((lat_h[...], lat_l[...]), block_ref[...]) * SCALING
    modes_ref[...] = modes
    direct = jnp.zeros((32, 128), f32)
    crossed = jnp.zeros((32, 128), f32)
    for c in range(C):
        weight = unpack(first_ref, c)
        weights_ref[c] = weight
        direct = direct + spread(modes, c) * weight
        crossed = crossed + spread(modes, C + c) * weight
    mixed = (direct + times_i(crossed)) * depth_factor()
    out_ref[...] = lat_inverse((back_h[...], back_l[...]), mixed)


def mix_call(lat, block, first):
    return pl.pallas_call(
        mix_kernel,
        in_specs=[vmem()] * 6,
        out_specs=[vmem()] * 3,
        out_shape=[
            jax.ShapeDtypeStruct((NY, 128), f32),
            jax.ShapeDtypeStruct((32, 128), f32),
            jax.ShapeDtypeStruct((C, 32, 128), f32),
        ],
        compiler_params=params(),
    )(*lat, block, first)


def join_table():
    table = np.zeros((C, 2, 128, 128))
    for c in range(C):
        for part in range(2):
            for low in range(2):
                table[c, part, 64 * low : 64 * low + 2 * C, 64 * low + C * part + c] = 1
    return table.reshape(2 * 128 * C, 128)


def adjoint_kernel(
    lat_h, lat_l, back_h, back_l, join_ref, block_ref, weights_ref, out_ref, grad_ref
):
    grad = lat_forward((lat_h[...], lat_l[...]), block_ref[...]) * depth_factor()
    grad_ref[...] = grad
    crossed = -times_i(grad)
    terms = []
    for c in range(C):
        weight = weights_ref[c]
        terms += [weight * grad, weight * crossed]
    high, low = split(jnp.concatenate(terms, 1))
    both = dot(jnp.concatenate([high, low], 0), join_ref[...])
    block = both[:32] + both[32:]
    out_ref[...] = lat_inverse((back_h[...], back_l[...]), block * SCALING)


def adjoint_call(lat, joins, block, weights):
    return pl.pallas_call(
        adjoint_kernel,
        in_specs=[vmem()] * 7,
        out_specs=[vmem()] * 2,
        out_shape=[
            jax.ShapeDtypeStruct((NY, 128), f32),
            jax.ShapeDtypeStruct((32, 128), f32),
        ],
        compiler_params=params(),
    )(*lat, joins, block, weights)


ROOT = math.sqrt(2.0 / math.pi)
CUBE = 0.044715


def bypass_blocks(bypass, dims):
    row = lax.broadcasted_iota(jnp.int32, (8 * C, C), 0)
    column = lax.broadcasted_iota(jnp.int32, (8 * C, C), 1)
    select = (row // 8 == column).astype(f32).astype(bf16)
    row = lax.broadcasted_iota(jnp.int32, (8 * C, 8 * C), 0)
    column = lax.broadcasted_iota(jnp.int32, (8 * C, 8 * C), 1)
    same = row % 8 == column % 8
    blocks = []
    for half in split(bypass):
        wide = dot(dot(select, half, dims).astype(bf16), select, ((1,), (1,)))
        blocks.append(jnp.where(same, wide, 0.0))
    return jnp.concatenate(blocks, 0).astype(bf16)


def bypass_product(blocks, values):
    high, low = split(values)
    tall = dot(blocks, high)
    return tall[: 8 * C] + tall[8 * C :] + dot(blocks[: 8 * C], low)


def bypass_rows(bypass, dims, values_ref, field):
    blocks = bypass_blocks(bypass, dims)
    for y in range(YL):
        for half in range(2):
            rows = slice(8 * half, 8 * half + 8)
            place = slice(y * ZL + 8 * half, y * ZL + 8 * half + 8)
            values = values_ref[:, y, rows, :].reshape(8 * C, NX)
            field[:, place, :] = bypass_product(blocks, values).reshape(C, 8, NX)


def layer_kernel(
    back_ref, deep, bypass_ref, bias_hbm, block_ref, values_ref, cot_ref, out_hbm, slope_ref,
    send_ref, bias, field, outs, coef, coef_next, small_sems, sems
):
    fetch = Fetch(small_sems)
    bias_copy = fetch.start(bias_hbm, bias)

    def out_copy(channel):
        return pltpu.make_async_copy(outs.at[channel], out_hbm.at[channel], sems.at[channel])

    bypass_rows(bypass_ref[...], ((1,), (1,)), values_ref, field)
    deep_inverse(deep, block_ref, coef)
    bias_copy.wait()
    for step in range(C // PAIR):
        slopes = []
        for channel in range(PAIR * step, PAIR * step + PAIR):
            before = wide_inverse(coef, back_ref[...], channel) + field[channel] + bias[channel]
            square = before * before
            bend = jnp.tanh(before * (ROOT + (ROOT * CUBE) * square))
            half_up = 0.5 + 0.5 * bend
            rate = half_up + (half_up - half_up * half_up) * before * (
                2.0 * ROOT + (6.0 * ROOT * CUBE) * square
            )
            slope = cot_ref[channel].reshape(LANES, NX) * rate
            outs[channel] = (before * half_up).reshape(YL, ZL, NX)
            out_copy(channel).start()
            slope_ref[channel] = slope.reshape(YL, ZL, NX)
            slopes.append(slope)
        wide_forward(deep[DEEP_ROWS:, : 2 * LANES], jnp.concatenate(slopes, 0), coef_next, PAIR * step)
    clear_extra(coef_next)
    deep_forward(deep, coef_next, send_ref)
    for channel in range(C):
        out_copy(channel).wait()


def grid_shape():
    return jax.ShapeDtypeStruct((C, YL, ZL, NX), f32)


def grid_buffer():
    return pltpu.VMEM((C, YL, ZL, NX), f32)


def layer_call(back, deep, bypass, bias, block, values, cotangent):
    return pl.pallas_call(
        layer_kernel,
        in_specs=[vmem(), vmem(), vmem(), anywhere(), vmem(), vmem(), vmem()],
        out_specs=[anywhere(), vmem(), vmem()],
        out_shape=[
            grid_shape(),
            grid_shape(),
            jax.ShapeDtypeStruct((GZ, SEND_ROWS, 128), f32),
        ],
        scratch_shapes=[
            pltpu.SMEM((C,), f32),
            pltpu.VMEM((C, LANES, NX), f32),
            grid_buffer(),
            pltpu.VMEM((COEF_ROWS, LANES), f32),
            pltpu.VMEM((COEF_ROWS, LANES), f32),
            pltpu.SemaphoreType.DMA((2,)),
            pltpu.SemaphoreType.DMA((C,)),
        ],
        compiler_params=params(WIDE_LIMIT),
    )(back, deep, bypass, bias, block, values, cotangent)


def last_kernel(
    back_ref, deep, bypass_ref, block_ref, slope_ref, out_hbm, weight_hbm, field, outs, coef,
    weight, modes_rows, grad_rows, small_sems, sems
):
    fetch = Fetch(small_sems)

    def out_copy(y):
        return pltpu.make_async_copy(outs.at[:, y], out_hbm.at[:, y], sems.at[y])

    for ky in range(4):
        for low in range(2):
            rows = pl.ds(low, GZ, stride=2)
            modes_rows[rows, :] = turn(block_ref[:, SEND_ROWS + ky, :], 64 * low)
            grad_rows[rows, :] = turn(block_ref[:, SEND_ROWS + 4 + ky, :], 64 * low)
        modes = modes_rows[...]
        grad_real = grad_rows[...]
        grad_imag = turn(grad_real, -C)
        for channel in range(C):
            real = modes[:, channel : channel + 1]
            imag = modes[:, C + channel : C + channel + 1]
            weight[channel, ky] = (real * grad_real + imag * grad_imag)[:, :C]
            weight[channel, 4 + ky] = (real * grad_imag - imag * grad_real)[:, :C]
    weight_copy = fetch.start(weight, weight_hbm)
    deep_inverse(deep, block_ref, coef)
    for channel in range(C):
        field[channel] = wide_inverse(coef, back_ref[...], channel)
    blocks = bypass_blocks(bypass_ref[...], ((1,), (0,)))
    for y in range(YL):
        for half in range(2):
            rows = slice(8 * half, 8 * half + 8)
            place = slice(y * ZL + 8 * half, y * ZL + 8 * half + 8)
            slopes = slope_ref[:, y, rows, :].reshape(8 * C, NX)
            total = bypass_product(blocks, slopes) + field[:, place, :].reshape(8 * C, NX)
            outs[:, y, rows, :] = total.reshape(C, 8, NX)
        out_copy(y).start()
    for y in range(YL):
        out_copy(y).wait()
    weight_copy.wait()


def last_call(back, deep, bypass, block, slopes):
    weight_shape = (C, 8, MODES, C)
    return pl.pallas_call(
        last_kernel,
        in_specs=[vmem()] * 5,
        out_specs=[anywhere(), anywhere()],
        out_shape=[grid_shape(), jax.ShapeDtypeStruct(weight_shape, f32)],
        scratch_shapes=[
            pltpu.VMEM((C, LANES, NX), f32),
            grid_buffer(),
            pltpu.VMEM((COEF_ROWS, LANES), f32),
            pltpu.VMEM(weight_shape, f32),
            pltpu.VMEM((MODES, 128), f32),
            pltpu.VMEM((MODES, 128), f32),
            pltpu.SemaphoreType.DMA((1,)),
            pltpu.SemaphoreType.DMA((YL,)),
        ],
        compiler_params=params(WIDE_LIMIT),
    )(back, deep, bypass, block, slopes)


def exchange(block, axis):
    return lax.all_to_all(block, axis, split_axis=0, concat_axis=0, tiled=True)


def over_y(rows):
    return exchange(rows.reshape(GY, YL, 128), "gy").reshape(NY, 128)


def shards(grid_values, spectral_weights, bypass_weight, bias_vector, cotangent):
    wide_high, wide_low = halves(wide_table())
    nothing = np.zeros((8, NX), ml_dtypes.bfloat16)
    back = jnp.asarray(np.concatenate([wide_high, wide_low, wide_high, nothing], 0))
    deep_high, deep_low = halves(deep_table())
    deep = np.concatenate([deep_high, deep_low, deep_high], 3).reshape(GZ, DEEP_ROWS, 3 * LANES)
    wide = np.zeros((NX, 3 * LANES), ml_dtypes.bfloat16)
    wide[:, :KINDS] = wide_high.T
    wide[:, LANES : LANES + KINDS] = wide_low.T
    deep = np.concatenate([deep, np.broadcast_to(wide, (GZ,) + wide.shape)], 1)
    deep = jnp.asarray(deep)
    joins = jnp.asarray(join_table().astype(ml_dtypes.bfloat16))
    lat_full = lat_table()
    lat = tuple(jnp.asarray(t) for t in halves(lat_full) + halves(lat_full.T.copy()))
    weights = jnp.transpose(spectral_weights, (0, 2, 3, 4, 5, 1)).reshape(C, 8, MODES, C)
    values = grid_values.reshape(C, LANES, NX)

    sent, deep = first_call(deep, values, weights)
    first = exchange(sent, "gz")
    rows, modes, mixing = mix_call(lat, over_y(join_call(first)), first)
    got = lax.all_gather(fork_call(over_y(rows)), "gz", axis=0, tiled=True)
    output, slopes, sent = layer_call(
        back, deep, bypass_weight, bias_vector, got, grid_values, cotangent
    )

    got = exchange(sent, "gz")
    rows, grad = adjoint_call(lat, joins, over_y(join_call(got)), mixing)
    got = exchange(fork_call(over_y(rows), modes, grad), "gz")
    grad_values, weight_grad = last_call(back, deep, bypass_weight, got, slopes)
    weight_grad = weight_grad.reshape(C, 2, 1, 4, MODES, C)
    return output, grad_values, jnp.transpose(weight_grad, (0, 5, 1, 2, 3, 4))


def solution(mesh):
    in_specs = (
        P(None, "gy", "gz", None),
        P(None, None, None, "gy", "gz", None),
        P(),
        P(),
        P(None, "gy", "gz", None),
    )
    out_specs = (
        P(None, "gy", "gz", None),
        P(None, "gy", "gz", None),
        P(None, None, None, "gy", "gz", None),
    )
    return jax.shard_map(shards, mesh=mesh, in_specs=in_specs, out_specs=out_specs, check_vma=False)
```

```python
import math

import numpy as np
import ml_dtypes

import jax
import jax.numpy as jnp
from jax import lax
from jax.experimental import pallas as pl
from jax.experimental.pallas import tpu as pltpu
from jax.sharding import PartitionSpec as P

C = 20
NX = 256
NY = 256
NZ = 128
MODES = 16
GY = 32
GZ = 8
YL = NY // GY
ZL = NZ // GZ
LANES = YL * ZL
TILES = 5
SEND_ROWS = TILES * 32
WEIGHT_ROWS = 56
GRAD_ROWS = 64
EXTRA = 748
COEF_ROWS = 768
KINDS = 40

f32 = jnp.float32
bf16 = jnp.bfloat16
VMEM_LIMIT = 8 * 1024 * 1024
WIDE_LIMIT = 20 * 1024 * 1024
DEEP_ROWS = 2 * 2 * LANES

GROUPS = (0, 160, 320, 480)


def halves(array):
    high = array.astype(np.float32).astype(ml_dtypes.bfloat16)
    low = (array - high.astype(np.float64)).astype(np.float32).astype(ml_dtypes.bfloat16)
    return high, low


def wide_table():
    x = np.arange(NX)
    freq = np.concatenate([np.arange(16), np.arange(1, 17), [16]])
    angle = 2.0 * math.pi * ((freq[:, None] * x[None, :]) % NX) / NX
    table = np.zeros((KINDS, NX))
    table[:33] = np.cos(angle)
    table[16:32] = -np.sin(angle[16:32])
    return table


def deep_table():
    z = np.arange(NZ)
    kz = np.arange(MODES)
    angle = 2.0 * math.pi * ((kz[:, None] * z[None, :]) % NZ) / NZ
    cos, sin = np.cos(angle), np.sin(angle)
    both = np.stack([np.stack([cos, -sin], 1), np.stack([sin, cos], 1)], 0)
    both = both.reshape(2, MODES, 2, GZ, ZL)
    table = np.einsum("akrgz,yv->gakryvz", both, np.eye(YL))
    return table.reshape(GZ, 2, 2 * MODES * YL, LANES)


def lat_table():
    row = np.arange(2 * MODES)
    ky = 4 * (row % 8) + row // 8
    fy = np.where(ky < MODES, ky, ky - 2 * MODES)
    y = np.arange(NY)
    angle = 2.0 * math.pi * ((fy[:, None] * y[None, :]) % NY) / NY
    return np.concatenate([np.cos(angle), np.sin(angle)], 0)


def split(value):
    high = value.astype(bf16)
    low = (value - high.astype(f32)).astype(bf16)
    return high, low


def dot(left, right, dims=((1,), (0,))):
    return lax.dot_general(left, right, (dims, ((), ())), preferred_element_type=f32)


def dot3(left, right, dims=((1,), (0,))):
    return (
        dot(left[0], right[0], dims) + dot(left[0], right[1], dims) + dot(left[1], right[0], dims)
    )


def lane_index(shape):
    return lax.broadcasted_iota(jnp.int32, shape, len(shape) - 1)


def turn(value, amount):
    amount = amount % 128
    return value if amount == 0 else pltpu.roll(value, amount, 1)


def times_i(value):
    lane = lane_index(value.shape) % 64
    turned = jnp.where(lane < C, -turn(value, -C), turn(value, C))
    return jnp.where(lane < 2 * C, turned, 0.0)


PAIR = 2


def wide_forward(tables, values, coef_ref, channel):
    part = dot(jnp.concatenate(split(values), 1), tables)
    for n in range(values.shape[0] // LANES):
        rows = part[LANES * n : LANES * n + LANES].T
        rows = rows[:KINDS] + rows[64 : 64 + KINDS]
        for k, start in enumerate(GROUPS):
            coef_ref[pl.ds(start + channel + n, 8, stride=C), :] = rows[8 * k : 8 * k + 8]
        coef_ref[pl.ds(EXTRA + channel + n, 1), :] = rows[32:33]


def wide_inverse(coef_ref, table, channel):
    rows = [coef_ref[pl.ds(start + channel, 8, stride=C), :] for start in GROUPS]
    rows.append(coef_ref[pl.ds(EXTRA + channel, 1), :])
    rows.append(jnp.zeros((7, LANES), f32))
    coef = jnp.concatenate(rows, 0)
    high = coef.astype(bf16).astype(f32)
    stacked = jnp.concatenate([high, high, coef - high, jnp.zeros((8, LANES), f32)], 0)
    return dot(stacked.T.astype(bf16), table)


def clear_extra(coef_ref):
    coef_ref[640:EXTRA, :] = jnp.zeros((EXTRA - 640, LANES), f32)


def deep_forward(deep_ref, coef_ref, out_ref):
    def product(at, rows):
        high, low = split(rows)
        table = deep_ref[2 * LANES * at : 2 * LANES * at + 2 * LANES, :]
        return dot(table, jnp.concatenate([high, high, low], 1), ((1,), (1,)))

    real = product(0, jnp.concatenate([coef_ref[0:384, :], coef_ref[640:COEF_ROWS, :]], 0))
    imag = product(1, coef_ref[256:640, :])
    left = lane_index((2 * LANES, 128)) < 64
    tiles = (
        real[:, :128],
        real[:, 128:256],
        jnp.where(left, real[:, 256:384], imag[:, :128]),
        imag[:, 128:256],
        imag[:, 256:] - real[:, 384:],
    )
    for t, deep in enumerate(tiles):
        for g in range(GZ):
            out_ref[g, 32 * t : 32 * t + 32, :] = deep[32 * g : 32 * g + 32]


def deep_inverse(deep_ref, block_ref, coef_ref):
    def product(at, rows):
        high, low = split(rows)
        table = deep_ref[2 * LANES * at : 2 * LANES * at + 2 * LANES, : 2 * LANES]
        wide = dot(high, table)
        return wide[:, :LANES] + wide[:, LANES:] + dot(low, table[:, :LANES])

    sections = []
    for t in range(TILES):
        tile = jnp.concatenate([block_ref[g, 32 * t : 32 * t + 32, :] for g in range(GZ)], 0)
        sections.append(tile.T)
    rows = jnp.concatenate(sections, 0)
    real = product(0, jnp.concatenate([rows[:320], -rows[512:]], 0))
    coef_ref[0:320, :] = real[:320]
    coef_ref[640:COEF_ROWS, :] = real[320:]
    coef_ref[320:640, :] = product(1, rows[320:])


STEP_C = 10
OUT_C = 2
OUT_Y = 1
STEPS = C // STEP_C


class Fetch:
    def __init__(self, sems):
        self.sems = sems
        self.count = 0

    def start(self, source, target):
        copy = pltpu.make_async_copy(source, target, self.sems.at[self.count])
        self.count += 1
        copy.start()
        return copy


def fetch_deep(fetch, deep_hbm, deep):
    return fetch.start(deep_hbm.at[lax.axis_index("gz")], deep)


def pack_weights(weights_ref, out_ref):
    units = []
    for c in range(C):
        for ky in range(4):
            for low in range(2):
                for part in range(2):
                    units.append(weights_ref[c, part * 4 + ky, pl.ds(low, GZ, stride=2), :])
    for row in range(WEIGHT_ROWS):
        pieces = units[6 * row : 6 * row + 6]
        used = C * len(pieces)
        pieces.append(jnp.zeros((GZ, 128 - used), f32))
        out_ref[:, SEND_ROWS + row, :] = jnp.concatenate(pieces, 1)


def first_kernel(
    deep_hbm, tables_hbm, values_hbm, weights_hbm, out_ref, deep, tables, values, weights, coef,
    sems
):
    fetch = Fetch(sems)
    tables_copy = fetch.start(tables_hbm, tables)
    copies = []
    for k in range(STEPS):
        part = pl.ds(k * STEP_C, STEP_C)
        copies.append(fetch.start(values_hbm.at[part], values.at[part]))
    deep_copy = fetch_deep(fetch, deep_hbm, deep)
    weights_copy = fetch.start(weights_hbm, weights)
    clear_extra(coef)
    tables_copy.wait()
    for k in range(STEPS):
        copies[k].wait()
        for channel in range(k * STEP_C, k * STEP_C + STEP_C, PAIR):
            both = values[channel : channel + PAIR].reshape(PAIR * LANES, NX)
            wide_forward(tables[...], both, coef, channel)
    weights_copy.wait()
    pack_weights(weights, out_ref)
    deep_copy.wait()
    deep_forward(deep, coef, out_ref)


def anywhere():
    return pl.BlockSpec(memory_space=pl.ANY)


def vmem():
    return pl.BlockSpec(memory_space=pltpu.VMEM)


def params(limit=VMEM_LIMIT):
    return pltpu.CompilerParams(vmem_limit_bytes=limit)


def first_call(deep, tables, values, weights):
    shape = (GZ, SEND_ROWS + WEIGHT_ROWS, 128)
    operands = (deep, tables, values, weights)
    return pl.pallas_call(
        first_kernel,
        in_specs=[pl.BlockSpec(memory_space=pltpu.HBM)] * len(operands),
        out_specs=[vmem()] * 3,
        out_shape=[
            jax.ShapeDtypeStruct(shape, f32),
            jax.ShapeDtypeStruct(deep.shape[1:], bf16),
            jax.ShapeDtypeStruct(tables.shape, bf16),
        ],
        scratch_shapes=[
            pltpu.VMEM(values.shape, f32),
            pltpu.VMEM(weights.shape, f32),
            pltpu.VMEM((COEF_ROWS, LANES), f32),
            pltpu.SemaphoreType.DMA((STEPS + 3,)),
        ],
        compiler_params=params(WIDE_LIMIT),
    )(*(pltpu.with_memory_space_constraint(a, pltpu.HBM) for a in operands))


def join_kernel(block_ref, out_ref):
    tiles = []
    for t in range(TILES):
        rows = slice(32 * t, 32 * t + 32)
        total = block_ref[0, rows, :]
        for g in range(1, GZ):
            total = total + block_ref[g, rows, :]
        tiles.append(total)
    joined = jnp.concatenate(tiles, 1)
    gap = jnp.zeros((YL, 64 - 2 * C), f32)

    def arranged(at):
        cut = joined[:, C * at : C * at + C]
        return jnp.concatenate([cut[0:8], cut[8:16], gap, cut[16:24], cut[24:32], gap], 1)

    out_ref[0:8, :] = arranged(0)
    for f in range(1, 16):
        real = arranged(f)
        imag = arranged(15 + f)
        out_ref[8 * f : 8 * f + 8, :] = real + imag
        out_ref[8 * (32 - f) : 8 * (32 - f) + 8, :] = real - imag
    out_ref[128:136, :] = -arranged(31)


def join_call(block):
    return pl.pallas_call(
        join_kernel,
        in_specs=[vmem()],
        out_specs=vmem(),
        out_shape=jax.ShapeDtypeStruct((NY, 128), f32),
        compiler_params=params(),
    )(block)


def fork_blocks(block_ref, out_ref):
    blocks = [block_ref[0:8, :]]
    differences = []
    for f in range(1, 16):
        plus = block_ref[8 * f : 8 * f + 8, :]
        minus = block_ref[8 * (32 - f) : 8 * (32 - f) + 8, :]
        blocks.append(plus + minus)
        differences.append(plus - minus)
    blocks = blocks + differences + [-block_ref[128:136, :]]
    for k in range(4):
        lane = 64 * (k // 2) + C * (k % 2)
        row = jnp.concatenate([b[:, lane : lane + C] for b in blocks], 1)
        for t in range(TILES):
            out_ref[0, 32 * t + 8 * k : 32 * t + 8 * k + 8, :] = row[:, 128 * t : 128 * t + 128]


def fork_kernel(block_ref, out_ref):
    fork_blocks(block_ref, out_ref)


def fork_grads_kernel(block_ref, modes_ref, grad_ref, out_ref):
    fork_blocks(block_ref, out_ref)
    out_ref[0, SEND_ROWS : SEND_ROWS + 32, :] = modes_ref[...]
    out_ref[0, SEND_ROWS + 32 :, :] = grad_ref[...]


def fork_call(block, *grads):
    rows = SEND_ROWS + (GRAD_ROWS if grads else 0)
    return pl.pallas_call(
        fork_grads_kernel if grads else fork_kernel,
        in_specs=[vmem()] * (1 + len(grads)),
        out_specs=vmem(),
        out_shape=jax.ShapeDtypeStruct((1, rows, 128), f32),
        compiler_params=params(),
    )(block, *grads)


def unpack(block_ref, c):
    left = lane_index((GZ, 128)) < 64
    rows = []
    loaded = {}
    for ky in range(4):
        sides = []
        for low in range(2):
            unit = (c * 4 + ky) * 2 + low
            row = SEND_ROWS + unit // 3
            if row not in loaded:
                loaded[row] = block_ref[:, row, :]
            sides.append(turn(loaded[row], 64 * low - 40 * (unit % 3)))
        rows.append(jnp.where(left, sides[0], sides[1]))
    return jnp.concatenate(rows, 0)


def lat_forward(lat, block):
    both = dot3(lat, split(block))
    return both[:32] - times_i(both[32:])


def lat_inverse(lat_back, modes):
    return dot3(lat_back, split(jnp.concatenate([modes, times_i(modes)], 0)))


def spread(modes, lane):
    left = lane_index(modes.shape) < 64
    return jnp.where(left, modes[:, lane : lane + 1], modes[:, 64 + lane : 65 + lane])


SCALING = 1.0 / math.sqrt(NX * NY * NZ)


def depth_factor():
    lane = lane_index((32, 128))
    first = (lane < 64) & (lax.axis_index("gz") == 0)
    scale = 1.0 / (2.0 * math.sqrt(4.0 * MODES * MODES * MODES))
    factor = jnp.where(first, f32(scale), f32(2.0 * scale))
    return jnp.where(lane % 64 < 2 * C, factor, 0.0)


def mix_kernel(
    lat_h, lat_l, back_h, back_l, block_ref, first_ref, out_ref, modes_ref, weights_ref
):
    modes = lat_forward((lat_h[...], lat_l[...]), block_ref[...]) * SCALING
    modes_ref[...] = modes
    direct = jnp.zeros((32, 128), f32)
    crossed = jnp.zeros((32, 128), f32)
    for c in range(C):
        weight = unpack(first_ref, c)
        weights_ref[c] = weight
        direct = direct + spread(modes, c) * weight
        crossed = crossed + spread(modes, C + c) * weight
    mixed = (direct + times_i(crossed)) * depth_factor()
    out_ref[...] = lat_inverse((back_h[...], back_l[...]), mixed)


def mix_call(lat, block, first):
    return pl.pallas_call(
        mix_kernel,
        in_specs=[vmem()] * 6,
        out_specs=[vmem()] * 3,
        out_shape=[
            jax.ShapeDtypeStruct((NY, 128), f32),
            jax.ShapeDtypeStruct((32, 128), f32),
            jax.ShapeDtypeStruct((C, 32, 128), f32),
        ],
        compiler_params=params(),
    )(*lat, block, first)


def join_table():
    table = np.zeros((C, 2, 128, 128))
    for c in range(C):
        for part in range(2):
            for low in range(2):
                table[c, part, 64 * low : 64 * low + 2 * C, 64 * low + C * part + c] = 1
    return table.reshape(2 * 128 * C, 128)


def adjoint_kernel(
    lat_h, lat_l, back_h, back_l, join_ref, block_ref, weights_ref, out_ref, grad_ref
):
    grad = lat_forward((lat_h[...], lat_l[...]), block_ref[...]) * depth_factor()
    grad_ref[...] = grad
    crossed = -times_i(grad)
    terms = []
    for c in range(C):
        weight = weights_ref[c]
        terms += [weight * grad, weight * crossed]
    high, low = split(jnp.concatenate(terms, 1))
    both = dot(jnp.concatenate([high, low], 0), join_ref[...])
    block = both[:32] + both[32:]
    out_ref[...] = lat_inverse((back_h[...], back_l[...]), block * SCALING)


def adjoint_call(lat, joins, block, weights):
    return pl.pallas_call(
        adjoint_kernel,
        in_specs=[vmem()] * 7,
        out_specs=[vmem()] * 2,
        out_shape=[
            jax.ShapeDtypeStruct((NY, 128), f32),
            jax.ShapeDtypeStruct((32, 128), f32),
        ],
        compiler_params=params(),
    )(*lat, joins, block, weights)


ROOT = math.sqrt(2.0 / math.pi)
CUBE = 0.044715


def bypass_blocks(bypass, dims):
    row = lax.broadcasted_iota(jnp.int32, (8 * C, C), 0)
    column = lax.broadcasted_iota(jnp.int32, (8 * C, C), 1)
    select = (row // 8 == column).astype(f32).astype(bf16)
    row = lax.broadcasted_iota(jnp.int32, (8 * C, 8 * C), 0)
    column = lax.broadcasted_iota(jnp.int32, (8 * C, 8 * C), 1)
    same = row % 8 == column % 8
    blocks = []
    for half in split(bypass):
        wide = dot(dot(select, half, dims).astype(bf16), select, ((1,), (1,)))
        blocks.append(jnp.where(same, wide, 0.0))
    return jnp.concatenate([blocks[0], blocks[1], blocks[0]], 1).astype(bf16)


def bypass_product(blocks, values):
    high, low = split(values)
    return dot(blocks, jnp.concatenate([high, high, low], 0))


def bypass_rows(bypass, dims, values_ref, field):
    blocks = bypass_blocks(bypass, dims)
    for y in range(YL):
        for half in range(2):
            rows = slice(8 * half, 8 * half + 8)
            place = slice(y * ZL + 8 * half, y * ZL + 8 * half + 8)
            values = values_ref[:, y, rows, :].reshape(8 * C, NX)
            field[:, place, :] = bypass_product(blocks, values).reshape(C, 8, NX)


def layer_kernel(
    back_ref, deep, tables_ref, bypass_ref, bias_hbm, block_ref, values_ref, cot_ref, out_hbm, slope_ref,
    send_ref, bias, field, outs, coef, coef_next, small_sems, sems
):
    fetch = Fetch(small_sems)
    bias_copy = fetch.start(bias_hbm, bias)

    def out_copy(part):
        group = pl.ds(part * OUT_C, OUT_C)
        return pltpu.make_async_copy(outs.at[group], out_hbm.at[group], sems.at[part])

    bypass_rows(bypass_ref[...], ((1,), (1,)), values_ref, field)
    deep_inverse(deep, block_ref, coef)
    bias_copy.wait()
    for step in range(C // PAIR):
        slopes = []
        for channel in range(PAIR * step, PAIR * step + PAIR):
            before = wide_inverse(coef, back_ref[...], channel) + field[channel] + bias[channel]
            square = before * before
            bend = jnp.tanh(before * (ROOT + (ROOT * CUBE) * square))
            half_up = 0.5 + 0.5 * bend
            rate = half_up + (half_up - half_up * half_up) * before * (
                2.0 * ROOT + (6.0 * ROOT * CUBE) * square
            )
            slope = cot_ref[channel].reshape(LANES, NX) * rate
            outs[channel] = (before * half_up).reshape(YL, ZL, NX)
            if channel % OUT_C == OUT_C - 1:
                out_copy(channel // OUT_C).start()
            slope_ref[channel] = slope.reshape(YL, ZL, NX)
            slopes.append(slope)
        wide_forward(tables_ref[...], jnp.concatenate(slopes, 0), coef_next, PAIR * step)
    clear_extra(coef_next)
    deep_forward(deep, coef_next, send_ref)
    for part in range(C // OUT_C):
        out_copy(part).wait()


def grid_shape():
    return jax.ShapeDtypeStruct((C, YL, ZL, NX), f32)


def grid_buffer():
    return pltpu.VMEM((C, YL, ZL, NX), f32)


def layer_call(back, deep, tables, bypass, bias, block, values, cotangent):
    return pl.pallas_call(
        layer_kernel,
        in_specs=[vmem()] * 4 + [anywhere()] + [vmem()] * 3,
        out_specs=[anywhere(), vmem(), vmem()],
        out_shape=[
            grid_shape(),
            grid_shape(),
            jax.ShapeDtypeStruct((GZ, SEND_ROWS, 128), f32),
        ],
        scratch_shapes=[
            pltpu.SMEM((C,), f32),
            pltpu.VMEM((C, LANES, NX), f32),
            grid_buffer(),
            pltpu.VMEM((COEF_ROWS, LANES), f32),
            pltpu.VMEM((COEF_ROWS, LANES), f32),
            pltpu.SemaphoreType.DMA((2,)),
            pltpu.SemaphoreType.DMA((C // OUT_C,)),
        ],
        compiler_params=params(WIDE_LIMIT),
    )(back, deep, tables, bypass, bias, block, values, cotangent)


def last_kernel(
    back_ref, deep, bypass_ref, block_ref, slope_ref, out_hbm, weight_hbm, field, outs, coef,
    weight, modes_rows, grad_rows, small_sems, sems
):
    fetch = Fetch(small_sems)

    def out_copy(part):
        rows = pl.ds(part * OUT_Y, OUT_Y)
        return pltpu.make_async_copy(outs.at[:, rows], out_hbm.at[:, rows], sems.at[part])

    for ky in range(4):
        for low in range(2):
            rows = pl.ds(low, GZ, stride=2)
            own = SEND_ROWS + 8 * ky + lax.axis_index("gz")
            modes_rows[rows, :] = turn(block_ref[:, pl.ds(own, 1), :].reshape(GZ, 128), 64 * low)
            own = own + 32
            grad_rows[rows, :] = turn(block_ref[:, pl.ds(own, 1), :].reshape(GZ, 128), 64 * low)
        modes = modes_rows[...]
        grad_real = grad_rows[...]
        grad_imag = turn(grad_real, -C)
        for channel in range(C):
            real = modes[:, channel : channel + 1]
            imag = modes[:, C + channel : C + channel + 1]
            weight[channel, ky] = (real * grad_real + imag * grad_imag)[:, :C]
            weight[channel, 4 + ky] = (real * grad_imag - imag * grad_real)[:, :C]
    weight_copy = fetch.start(weight, weight_hbm)
    deep_inverse(deep, block_ref, coef)
    for channel in range(C):
        field[channel] = wide_inverse(coef, back_ref[...], channel)
    blocks = bypass_blocks(bypass_ref[...], ((1,), (0,)))
    for y in range(YL):
        for half in range(2):
            rows = slice(8 * half, 8 * half + 8)
            place = slice(y * ZL + 8 * half, y * ZL + 8 * half + 8)
            slopes = slope_ref[:, y, rows, :].reshape(8 * C, NX)
            total = bypass_product(blocks, slopes) + field[:, place, :].reshape(8 * C, NX)
            outs[:, y, rows, :] = total.reshape(C, 8, NX)
        if y % OUT_Y == OUT_Y - 1:
            out_copy(y // OUT_Y).start()
    for part in range(YL // OUT_Y):
        out_copy(part).wait()
    weight_copy.wait()


def last_call(back, deep, bypass, block, slopes):
    weight_shape = (C, 8, MODES, C)
    return pl.pallas_call(
        last_kernel,
        in_specs=[vmem()] * 5,
        out_specs=[anywhere(), anywhere()],
        out_shape=[grid_shape(), jax.ShapeDtypeStruct(weight_shape, f32)],
        scratch_shapes=[
            pltpu.VMEM((C, LANES, NX), f32),
            grid_buffer(),
            pltpu.VMEM((COEF_ROWS, LANES), f32),
            pltpu.VMEM(weight_shape, f32),
            pltpu.VMEM((MODES, 128), f32),
            pltpu.VMEM((MODES, 128), f32),
            pltpu.SemaphoreType.DMA((1,)),
            pltpu.SemaphoreType.DMA((YL // OUT_Y,)),
        ],
        compiler_params=params(WIDE_LIMIT),
    )(back, deep, bypass, block, slopes)


def exchange(block, axis):
    return lax.all_to_all(block, axis, split_axis=0, concat_axis=0, tiled=True)


def gather(block):
    return lax.all_gather(block, "gz", axis=0, tiled=True)


def over_y(rows):
    return exchange(rows.reshape(GY, YL, 128), "gy").reshape(NY, 128)


def shards(grid_values, spectral_weights, bypass_weight, bias_vector, cotangent):
    wide_high, wide_low = halves(wide_table())
    nothing = np.zeros((8, NX), ml_dtypes.bfloat16)
    back = jnp.asarray(np.concatenate([wide_high, wide_low, wide_high, nothing], 0))
    deep_high, deep_low = halves(deep_table())
    deep = np.concatenate([deep_high, deep_low, deep_high], 3).reshape(GZ, DEEP_ROWS, 3 * LANES)
    tables = np.zeros((2 * NX, LANES), ml_dtypes.bfloat16)
    tables[:NX, :KINDS] = wide_high.T
    tables[:NX, 64 : 64 + KINDS] = wide_low.T
    tables[NX:, :KINDS] = wide_high.T
    deep = jnp.asarray(deep)
    tables = jnp.asarray(tables)
    joins = jnp.asarray(join_table().astype(ml_dtypes.bfloat16))
    lat_full = lat_table()
    lat = tuple(jnp.asarray(t) for t in halves(lat_full) + halves(lat_full.T.copy()))
    weights = jnp.transpose(spectral_weights, (0, 2, 3, 4, 5, 1)).reshape(C, 8, MODES, C)
    values = grid_values.reshape(C, LANES, NX)

    sent, deep, tables = first_call(deep, tables, values, weights)
    first = exchange(sent, "gz")
    rows, modes, mixing = mix_call(lat, over_y(join_call(first)), first)
    got = gather(fork_call(over_y(rows)))
    output, slopes, sent = layer_call(
        back, deep, tables, bypass_weight, bias_vector, got, grid_values, cotangent
    )

    got = exchange(sent, "gz")
    rows, grad = adjoint_call(lat, joins, over_y(join_call(got)), mixing)
    got = gather(fork_call(over_y(rows), modes, grad))
    grad_values, weight_grad = last_call(back, deep, bypass_weight, got, slopes)
    weight_grad = weight_grad.reshape(C, 2, 1, 4, MODES, C)
    return output, grad_values, jnp.transpose(weight_grad, (0, 5, 1, 2, 3, 4))


def solution(mesh):
    in_specs = (
        P(None, "gy", "gz", None),
        P(None, None, None, "gy", "gz", None),
        P(),
        P(),
        P(None, "gy", "gz", None),
    )
    out_specs = (
        P(None, "gy", "gz", None),
        P(None, "gy", "gz", None),
        P(None, None, None, "gy", "gz", None),
    )
    return jax.shard_map(shards, mesh=mesh, in_specs=in_specs, out_specs=out_specs, check_vma=False)
```

```python
import math

import numpy as np
import ml_dtypes

import jax
import jax.numpy as jnp
from jax import lax
from jax.experimental import pallas as pl
from jax.experimental.pallas import tpu as pltpu
from jax.sharding import PartitionSpec as P

C = 20
NX = 256
NY = 256
NZ = 128
MODES = 16
GY = 32
GZ = 8
YL = NY // GY
ZL = NZ // GZ
LANES = YL * ZL
TILES = 5
SEND_ROWS = TILES * 32
WEIGHT_ROWS = 56
GRAD_ROWS = 64
EXTRA = 748
COEF_ROWS = 768
KINDS = 40

f32 = jnp.float32
bf16 = jnp.bfloat16
VMEM_LIMIT = 8 * 1024 * 1024
WIDE_LIMIT = 20 * 1024 * 1024
DEEP_ROWS = 2 * 2 * LANES

GROUPS = (0, 160, 320, 480)


def halves(array):
    high = array.astype(np.float32).astype(ml_dtypes.bfloat16)
    low = (array - high.astype(np.float64)).astype(np.float32).astype(ml_dtypes.bfloat16)
    return high, low


def wide_table():
    x = np.arange(NX)
    freq = np.concatenate([np.arange(16), np.arange(1, 17), [16]])
    angle = 2.0 * math.pi * ((freq[:, None] * x[None, :]) % NX) / NX
    table = np.zeros((KINDS, NX))
    table[:33] = np.cos(angle)
    table[16:32] = -np.sin(angle[16:32])
    return table


def deep_table():
    z = np.arange(NZ)
    kz = np.arange(MODES)
    angle = 2.0 * math.pi * ((kz[:, None] * z[None, :]) % NZ) / NZ
    cos, sin = np.cos(angle), np.sin(angle)
    both = np.stack([np.stack([cos, -sin], 1), np.stack([sin, cos], 1)], 0)
    both = both.reshape(2, MODES, 2, GZ, ZL)
    table = np.einsum("akrgz,yv->gakryvz", both, np.eye(YL))
    return table.reshape(GZ, 2, 2 * MODES * YL, LANES)


def lat_table():
    row = np.arange(2 * MODES)
    ky = 4 * (row % 8) + row // 8
    fy = np.where(ky < MODES, ky, ky - 2 * MODES)
    y = np.arange(NY)
    angle = 2.0 * math.pi * ((fy[:, None] * y[None, :]) % NY) / NY
    return np.concatenate([np.cos(angle), np.sin(angle)], 0)


def split(value):
    high = value.astype(bf16)
    low = (value - high.astype(f32)).astype(bf16)
    return high, low


def dot(left, right, dims=((1,), (0,))):
    return lax.dot_general(left, right, (dims, ((), ())), preferred_element_type=f32)


def dot3(left, right, dims=((1,), (0,))):
    return (
        dot(left[0], right[0], dims) + dot(left[0], right[1], dims) + dot(left[1], right[0], dims)
    )


def lane_index(shape):
    return lax.broadcasted_iota(jnp.int32, shape, len(shape) - 1)


def turn(value, amount):
    amount = amount % 128
    return value if amount == 0 else pltpu.roll(value, amount, 1)


def times_i(value):
    lane = lane_index(value.shape) % 64
    turned = jnp.where(lane < C, -turn(value, -C), turn(value, C))
    return jnp.where(lane < 2 * C, turned, 0.0)


PAIR = 2


def wide_forward(tables, values, coef_ref, channel):
    part = dot(jnp.concatenate(split(values), 1), tables)
    for n in range(values.shape[0] // LANES):
        rows = part[LANES * n : LANES * n + LANES].T
        rows = rows[:KINDS] + rows[64 : 64 + KINDS]
        for k, start in enumerate(GROUPS):
            coef_ref[pl.ds(start + channel + n, 8, stride=C), :] = rows[8 * k : 8 * k + 8]
        coef_ref[pl.ds(EXTRA + channel + n, 1), :] = rows[32:33]


def wide_inverse(coef_ref, table, channel):
    rows = [coef_ref[pl.ds(start + channel, 8, stride=C), :] for start in GROUPS]
    rows.append(coef_ref[pl.ds(EXTRA + channel, 1), :])
    rows.append(jnp.zeros((7, LANES), f32))
    coef = jnp.concatenate(rows, 0)
    high = coef.astype(bf16).astype(f32)
    stacked = jnp.concatenate([high, high, coef - high, jnp.zeros((8, LANES), f32)], 0)
    return dot(stacked.T.astype(bf16), table)


def clear_extra(coef_ref):
    coef_ref[640:EXTRA, :] = jnp.zeros((EXTRA - 640, LANES), f32)


def deep_forward(deep_ref, coef_ref, out_ref):
    def product(at, rows):
        high, low = split(rows)
        table = deep_ref[2 * LANES * at : 2 * LANES * at + 2 * LANES, :]
        return dot(table, jnp.concatenate([high, high, low], 1), ((1,), (1,)))

    real = product(0, jnp.concatenate([coef_ref[0:384, :], coef_ref[640:COEF_ROWS, :]], 0))
    imag = product(1, coef_ref[256:640, :])
    left = lane_index((2 * LANES, 128)) < 64
    tiles = (
        real[:, :128],
        real[:, 128:256],
        jnp.where(left, real[:, 256:384], imag[:, :128]),
        imag[:, 128:256],
        imag[:, 256:] - real[:, 384:],
    )
    for t, deep in enumerate(tiles):
        for g in range(GZ):
            out_ref[g, 32 * t : 32 * t + 32, :] = deep[32 * g : 32 * g + 32]


def deep_inverse(deep_ref, block_ref, coef_ref):
    def product(at, rows):
        high, low = split(rows)
        table = deep_ref[2 * LANES * at : 2 * LANES * at + 2 * LANES, : 2 * LANES]
        wide = dot(high, table)
        return wide[:, :LANES] + wide[:, LANES:] + dot(low, table[:, :LANES])

    sections = []
    for t in range(TILES):
        tile = jnp.concatenate([block_ref[g, 32 * t : 32 * t + 32, :] for g in range(GZ)], 0)
        sections.append(tile.T)
    rows = jnp.concatenate(sections, 0)
    real = product(0, jnp.concatenate([rows[:320], -rows[512:]], 0))
    coef_ref[0:320, :] = real[:320]
    coef_ref[640:COEF_ROWS, :] = real[320:]
    coef_ref[320:640, :] = product(1, rows[320:])


STEP_C = 10
OUT_C = 2
OUT_Y = 1
STEPS = C // STEP_C


class Fetch:
    def __init__(self, sems):
        self.sems = sems
        self.count = 0

    def start(self, source, target):
        copy = pltpu.make_async_copy(source, target, self.sems.at[self.count])
        self.count += 1
        copy.start()
        return copy


def fetch_deep(fetch, deep_hbm, deep):
    return fetch.start(deep_hbm.at[lax.axis_index("gz")], deep)


def pack_weights(weights_ref, out_ref):
    units = []
    for c in range(C):
        for ky in range(4):
            for low in range(2):
                for part in range(2):
                    units.append(weights_ref[c, part * 4 + ky, pl.ds(low, GZ, stride=2), :])
    for row in range(WEIGHT_ROWS):
        pieces = units[6 * row : 6 * row + 6]
        used = C * len(pieces)
        pieces.append(jnp.zeros((GZ, 128 - used), f32))
        out_ref[:, SEND_ROWS + row, :] = jnp.concatenate(pieces, 1)


def first_kernel(
    deep_hbm, tables_hbm, values_hbm, weights_hbm, out_ref, deep, tables, values, weights, coef,
    sems
):
    fetch = Fetch(sems)
    tables_copy = fetch.start(tables_hbm, tables)
    copies = []
    for k in range(STEPS):
        part = pl.ds(k * STEP_C, STEP_C)
        copies.append(fetch.start(values_hbm.at[part], values.at[part]))
    deep_copy = fetch_deep(fetch, deep_hbm, deep)
    weights_copy = fetch.start(weights_hbm, weights)
    clear_extra(coef)
    tables_copy.wait()
    for k in range(STEPS):
        copies[k].wait()
        for channel in range(k * STEP_C, k * STEP_C + STEP_C, PAIR):
            both = values[channel : channel + PAIR].reshape(PAIR * LANES, NX)
            wide_forward(tables[...], both, coef, channel)
    weights_copy.wait()
    pack_weights(weights, out_ref)
    deep_copy.wait()
    deep_forward(deep, coef, out_ref)


def anywhere():
    return pl.BlockSpec(memory_space=pl.ANY)


def vmem():
    return pl.BlockSpec(memory_space=pltpu.VMEM)


def params(limit=VMEM_LIMIT):
    return pltpu.CompilerParams(vmem_limit_bytes=limit)


def first_call(deep, tables, values, weights):
    shape = (GZ, SEND_ROWS + WEIGHT_ROWS, 128)
    operands = (deep, tables, values, weights)
    return pl.pallas_call(
        first_kernel,
        in_specs=[pl.BlockSpec(memory_space=pltpu.HBM)] * len(operands),
        out_specs=[vmem()] * 3,
        out_shape=[
            jax.ShapeDtypeStruct(shape, f32),
            jax.ShapeDtypeStruct(deep.shape[1:], bf16),
            jax.ShapeDtypeStruct(tables.shape, bf16),
        ],
        scratch_shapes=[
            pltpu.VMEM(values.shape, f32),
            pltpu.VMEM(weights.shape, f32),
            pltpu.VMEM((COEF_ROWS, LANES), f32),
            pltpu.SemaphoreType.DMA((STEPS + 3,)),
        ],
        compiler_params=params(WIDE_LIMIT),
    )(*(pltpu.with_memory_space_constraint(a, pltpu.HBM) for a in operands))


def join_kernel(block_ref, out_ref):
    tiles = []
    for t in range(TILES):
        rows = slice(32 * t, 32 * t + 32)
        total = block_ref[0, rows, :]
        for g in range(1, GZ):
            total = total + block_ref[g, rows, :]
        tiles.append(total)
    joined = jnp.concatenate(tiles, 1)
    gap = jnp.zeros((YL, 64 - 2 * C), f32)

    def arranged(at):
        cut = joined[:, C * at : C * at + C]
        return jnp.concatenate([cut[0:8], cut[8:16], gap, cut[16:24], cut[24:32], gap], 1)

    out_ref[0:8, :] = arranged(0)
    for f in range(1, 16):
        real = arranged(f)
        imag = arranged(15 + f)
        out_ref[8 * f : 8 * f + 8, :] = real + imag
        out_ref[8 * (32 - f) : 8 * (32 - f) + 8, :] = real - imag
    out_ref[128:136, :] = -arranged(31)


def join_call(block):
    return pl.pallas_call(
        join_kernel,
        in_specs=[vmem()],
        out_specs=vmem(),
        out_shape=jax.ShapeDtypeStruct((NY, 128), f32),
        compiler_params=params(),
    )(block)


def fork_blocks(block_ref, out_ref):
    blocks = [block_ref[0:8, :]]
    differences = []
    for f in range(1, 16):
        plus = block_ref[8 * f : 8 * f + 8, :]
        minus = block_ref[8 * (32 - f) : 8 * (32 - f) + 8, :]
        blocks.append(plus + minus)
        differences.append(plus - minus)
    blocks = blocks + differences + [-block_ref[128:136, :]]
    for k in range(4):
        lane = 64 * (k // 2) + C * (k % 2)
        row = jnp.concatenate([b[:, lane : lane + C] for b in blocks], 1)
        for t in range(TILES):
            out_ref[0, 32 * t + 8 * k : 32 * t + 8 * k + 8, :] = row[:, 128 * t : 128 * t + 128]


def fork_kernel(block_ref, out_ref):
    fork_blocks(block_ref, out_ref)


def fork_grads_kernel(block_ref, modes_ref, grad_ref, out_ref):
    fork_blocks(block_ref, out_ref)
    out_ref[0, SEND_ROWS : SEND_ROWS + 32, :] = modes_ref[...]
    out_ref[0, SEND_ROWS + 32 :, :] = grad_ref[...]


def fork_call(block, *grads):
    rows = SEND_ROWS + (GRAD_ROWS if grads else 0)
    return pl.pallas_call(
        fork_grads_kernel if grads else fork_kernel,
        in_specs=[vmem()] * (1 + len(grads)),
        out_specs=vmem(),
        out_shape=jax.ShapeDtypeStruct((1, rows, 128), f32),
        compiler_params=params(),
    )(block, *grads)


def unpack(block_ref, c):
    left = lane_index((GZ, 128)) < 64
    rows = []
    loaded = {}
    for ky in range(4):
        sides = []
        for low in range(2):
            unit = (c * 4 + ky) * 2 + low
            row = SEND_ROWS + unit // 3
            if row not in loaded:
                loaded[row] = block_ref[:, row, :]
            sides.append(turn(loaded[row], 64 * low - 40 * (unit % 3)))
        rows.append(jnp.where(left, sides[0], sides[1]))
    return jnp.concatenate(rows, 0)


def stacked(value):
    high, low = split(value)
    return jnp.concatenate([high, high, low], 0)


def lat_forward(lat_ref, block):
    both = dot(lat_ref[...], stacked(block))
    return both[:32] - times_i(both[32:])


def lat_inverse(back_ref, modes):
    return dot(back_ref[...], stacked(jnp.concatenate([modes, times_i(modes)], 0)))


def spread_table():
    table = np.zeros((128, C, 2, 128))
    for c in range(C):
        for part in range(2):
            for low in range(2):
                table[64 * low + C * part + c, c, part, 64 * low : 64 * low + 64] = 1
    return table.reshape(128, 2 * 128 * C)


SCALING = 1.0 / math.sqrt(NX * NY * NZ)


def depth_factor():
    lane = lane_index((32, 128))
    first = (lane < 64) & (lax.axis_index("gz") == 0)
    scale = 1.0 / (2.0 * math.sqrt(4.0 * MODES * MODES * MODES))
    factor = jnp.where(first, f32(scale), f32(2.0 * scale))
    return jnp.where(lane % 64 < 2 * C, factor, 0.0)


def mix_kernel(
    lat_ref, inverse_ref, spread_ref, block_ref, first_ref, out_ref, modes_ref, weights_ref
):
    modes = lat_forward(lat_ref, block_ref[...]) * SCALING
    modes_ref[...] = modes
    both = dot(jnp.concatenate(split(modes), 0), spread_ref[...])
    wide = both[:32] + both[32:]
    direct = jnp.zeros((32, 128), f32)
    crossed = jnp.zeros((32, 128), f32)
    for c in range(C):
        weight = unpack(first_ref, c)
        weights_ref[c] = weight
        at = 256 * c
        direct = direct + wide[:, at : at + 128] * weight
        crossed = crossed + wide[:, at + 128 : at + 256] * weight
    mixed = (direct + times_i(crossed)) * depth_factor()
    out_ref[...] = lat_inverse(inverse_ref, mixed)


def mix_call(lat, spreads, block, first):
    return pl.pallas_call(
        mix_kernel,
        in_specs=[vmem()] * 5,
        out_specs=[vmem()] * 3,
        out_shape=[
            jax.ShapeDtypeStruct((NY, 128), f32),
            jax.ShapeDtypeStruct((32, 128), f32),
            jax.ShapeDtypeStruct((C, 32, 128), f32),
        ],
        compiler_params=params(),
    )(*lat, spreads, block, first)


def join_table():
    table = np.zeros((C, 2, 128, 128))
    for c in range(C):
        for part in range(2):
            for low in range(2):
                table[c, part, 64 * low : 64 * low + 2 * C, 64 * low + C * part + c] = 1
    return table.reshape(2 * 128 * C, 128)


def adjoint_kernel(
    lat_ref, inverse_ref, join_ref, block_ref, weights_ref, out_ref, grad_ref
):
    grad = lat_forward(lat_ref, block_ref[...]) * depth_factor()
    grad_ref[...] = grad
    crossed = -times_i(grad)
    terms = []
    for c in range(C):
        weight = weights_ref[c]
        terms += [weight * grad, weight * crossed]
    high, low = split(jnp.concatenate(terms, 1))
    both = dot(jnp.concatenate([high, low], 0), join_ref[...])
    block = both[:32] + both[32:]
    out_ref[...] = lat_inverse(inverse_ref, block * SCALING)


def adjoint_call(lat, joins, block, weights):
    return pl.pallas_call(
        adjoint_kernel,
        in_specs=[vmem()] * 5,
        out_specs=[vmem()] * 2,
        out_shape=[
            jax.ShapeDtypeStruct((NY, 128), f32),
            jax.ShapeDtypeStruct((32, 128), f32),
        ],
        compiler_params=params(),
    )(*lat, joins, block, weights)


ROOT = math.sqrt(2.0 / math.pi)
CUBE = 0.044715


def bypass_blocks(bypass, dims):
    row = lax.broadcasted_iota(jnp.int32, (8 * C, C), 0)
    column = lax.broadcasted_iota(jnp.int32, (8 * C, C), 1)
    select = (row // 8 == column).astype(f32).astype(bf16)
    row = lax.broadcasted_iota(jnp.int32, (8 * C, 8 * C), 0)
    column = lax.broadcasted_iota(jnp.int32, (8 * C, 8 * C), 1)
    same = row % 8 == column % 8
    blocks = []
    for half in split(bypass):
        wide = dot(dot(select, half, dims).astype(bf16), select, ((1,), (1,)))
        blocks.append(jnp.where(same, wide, 0.0))
    return jnp.concatenate([blocks[0], blocks[1], blocks[0]], 1).astype(bf16)


def bypass_product(blocks, values):
    high, low = split(values)
    return dot(blocks, jnp.concatenate([high, high, low], 0))


def bypass_rows(bypass, dims, values_ref, field):
    blocks = bypass_blocks(bypass, dims)
    for y in range(YL):
        for half in range(2):
            rows = slice(8 * half, 8 * half + 8)
            place = slice(y * ZL + 8 * half, y * ZL + 8 * half + 8)
            values = values_ref[:, y, rows, :].reshape(8 * C, NX)
            field[:, place, :] = bypass_product(blocks, values).reshape(C, 8, NX)


def layer_kernel(
    back_ref, deep, tables_ref, bypass_ref, bias_hbm, block_ref, values_ref, cot_ref, out_hbm, slope_ref,
    send_ref, bias, field, outs, coef, coef_next, small_sems, sems
):
    fetch = Fetch(small_sems)
    bias_copy = fetch.start(bias_hbm, bias)

    def out_copy(part):
        group = pl.ds(part * OUT_C, OUT_C)
        return pltpu.make_async_copy(outs.at[group], out_hbm.at[group], sems.at[part])

    bypass_rows(bypass_ref[...], ((1,), (1,)), values_ref, field)
    deep_inverse(deep, block_ref, coef)
    bias_copy.wait()
    for step in range(C // PAIR):
        slopes = []
        for channel in range(PAIR * step, PAIR * step + PAIR):
            before = wide_inverse(coef, back_ref[...], channel) + field[channel] + bias[channel]
            square = before * before
            bend = jnp.tanh(before * (ROOT + (ROOT * CUBE) * square))
            half_up = 0.5 + 0.5 * bend
            rate = half_up + (half_up - half_up * half_up) * before * (
                2.0 * ROOT + (6.0 * ROOT * CUBE) * square
            )
            slope = cot_ref[channel].reshape(LANES, NX) * rate
            outs[channel] = (before * half_up).reshape(YL, ZL, NX)
            if channel % OUT_C == OUT_C - 1:
                out_copy(channel // OUT_C).start()
            slope_ref[channel] = slope.reshape(YL, ZL, NX)
            slopes.append(slope)
        wide_forward(tables_ref[...], jnp.concatenate(slopes, 0), coef_next, PAIR * step)
    clear_extra(coef_next)
    deep_forward(deep, coef_next, send_ref)
    for part in range(C // OUT_C):
        out_copy(part).wait()


def grid_shape():
    return jax.ShapeDtypeStruct((C, YL, ZL, NX), f32)


def grid_buffer():
    return pltpu.VMEM((C, YL, ZL, NX), f32)


def layer_call(back, deep, tables, bypass, bias, block, values, cotangent):
    return pl.pallas_call(
        layer_kernel,
        in_specs=[vmem()] * 4 + [anywhere()] + [vmem()] * 3,
        out_specs=[anywhere(), vmem(), vmem()],
        out_shape=[
            grid_shape(),
            grid_shape(),
            jax.ShapeDtypeStruct((GZ, SEND_ROWS, 128), f32),
        ],
        scratch_shapes=[
            pltpu.SMEM((C,), f32),
            pltpu.VMEM((C, LANES, NX), f32),
            grid_buffer(),
            pltpu.VMEM((COEF_ROWS, LANES), f32),
            pltpu.VMEM((COEF_ROWS, LANES), f32),
            pltpu.SemaphoreType.DMA((2,)),
            pltpu.SemaphoreType.DMA((C // OUT_C,)),
        ],
        compiler_params=params(WIDE_LIMIT),
    )(back, deep, tables, bypass, bias, block, values, cotangent)


def last_kernel(
    back_ref, deep, bypass_ref, block_ref, slope_ref, out_hbm, weight_hbm, field, outs, coef,
    weight, modes_rows, grad_rows, small_sems, sems
):
    fetch = Fetch(small_sems)

    def out_copy(part):
        rows = pl.ds(part * OUT_Y, OUT_Y)
        return pltpu.make_async_copy(outs.at[:, rows], out_hbm.at[:, rows], sems.at[part])

    for ky in range(4):
        for low in range(2):
            rows = pl.ds(low, GZ, stride=2)
            own = SEND_ROWS + 8 * ky + lax.axis_index("gz")
            modes_rows[rows, :] = turn(block_ref[:, pl.ds(own, 1), :].reshape(GZ, 128), 64 * low)
            own = own + 32
            grad_rows[rows, :] = turn(block_ref[:, pl.ds(own, 1), :].reshape(GZ, 128), 64 * low)
        modes = modes_rows[...]
        grad_real = grad_rows[...]
        grad_imag = turn(grad_real, -C)
        for channel in range(C):
            real = modes[:, channel : channel + 1]
            imag = modes[:, C + channel : C + channel + 1]
            weight[channel, ky] = (real * grad_real + imag * grad_imag)[:, :C]
            weight[channel, 4 + ky] = (real * grad_imag - imag * grad_real)[:, :C]
    weight_copy = fetch.start(weight, weight_hbm)
    deep_inverse(deep, block_ref, coef)
    for channel in range(C):
        field[channel] = wide_inverse(coef, back_ref[...], channel)
    blocks = bypass_blocks(bypass_ref[...], ((1,), (0,)))
    for y in range(YL):
        for half in range(2):
            rows = slice(8 * half, 8 * half + 8)
            place = slice(y * ZL + 8 * half, y * ZL + 8 * half + 8)
            slopes = slope_ref[:, y, rows, :].reshape(8 * C, NX)
            total = bypass_product(blocks, slopes) + field[:, place, :].reshape(8 * C, NX)
            outs[:, y, rows, :] = total.reshape(C, 8, NX)
        if y % OUT_Y == OUT_Y - 1:
            out_copy(y // OUT_Y).start()
    for part in range(YL // OUT_Y):
        out_copy(part).wait()
    weight_copy.wait()


def last_call(back, deep, bypass, block, slopes):
    weight_shape = (C, 8, MODES, C)
    return pl.pallas_call(
        last_kernel,
        in_specs=[vmem()] * 5,
        out_specs=[anywhere(), anywhere()],
        out_shape=[grid_shape(), jax.ShapeDtypeStruct(weight_shape, f32)],
        scratch_shapes=[
            pltpu.VMEM((C, LANES, NX), f32),
            grid_buffer(),
            pltpu.VMEM((COEF_ROWS, LANES), f32),
            pltpu.VMEM(weight_shape, f32),
            pltpu.VMEM((MODES, 128), f32),
            pltpu.VMEM((MODES, 128), f32),
            pltpu.SemaphoreType.DMA((1,)),
            pltpu.SemaphoreType.DMA((YL // OUT_Y,)),
        ],
        compiler_params=params(WIDE_LIMIT),
    )(back, deep, bypass, block, slopes)


def exchange(block, axis):
    return lax.all_to_all(block, axis, split_axis=0, concat_axis=0, tiled=True)


def gather(block):
    return lax.all_gather(block, "gz", axis=0, tiled=True)


def over_y(rows):
    return exchange(rows.reshape(GY, YL, 128), "gy").reshape(NY, 128)


def shards(grid_values, spectral_weights, bypass_weight, bias_vector, cotangent):
    wide_high, wide_low = halves(wide_table())
    nothing = np.zeros((8, NX), ml_dtypes.bfloat16)
    back = jnp.asarray(np.concatenate([wide_high, wide_low, wide_high, nothing], 0))
    deep_high, deep_low = halves(deep_table())
    deep = np.concatenate([deep_high, deep_low, deep_high], 3).reshape(GZ, DEEP_ROWS, 3 * LANES)
    tables = np.zeros((2 * NX, LANES), ml_dtypes.bfloat16)
    tables[:NX, :KINDS] = wide_high.T
    tables[:NX, 64 : 64 + KINDS] = wide_low.T
    tables[NX:, :KINDS] = wide_high.T
    deep = jnp.asarray(deep)
    tables = jnp.asarray(tables)
    joins = jnp.asarray(join_table().astype(ml_dtypes.bfloat16))
    lat_full = lat_table()
    lat = tuple(
        jnp.asarray(np.concatenate([high, low, high], 1))
        for high, low in (halves(lat_full), halves(lat_full.T.copy()))
    )
    spreads = jnp.asarray(spread_table().astype(ml_dtypes.bfloat16))

    weights = jnp.transpose(spectral_weights, (0, 2, 3, 4, 5, 1)).reshape(C, 8, MODES, C)
    values = grid_values.reshape(C, LANES, NX)

    sent, deep, tables = first_call(deep, tables, values, weights)
    first = exchange(sent, "gz")
    rows, modes, mixing = mix_call(lat, spreads, over_y(join_call(first)), first)
    got = gather(fork_call(over_y(rows)))
    output, slopes, sent = layer_call(
        back, deep, tables, bypass_weight, bias_vector, got, grid_values, cotangent
    )

    got = exchange(sent, "gz")
    rows, grad = adjoint_call(lat, joins, over_y(join_call(got)), mixing)
    got = gather(fork_call(over_y(rows), modes, grad))
    grad_values, weight_grad = last_call(back, deep, bypass_weight, got, slopes)
    weight_grad = weight_grad.reshape(C, 2, 1, 4, MODES, C)
    return output, grad_values, jnp.transpose(weight_grad, (0, 5, 1, 2, 3, 4))


def solution(mesh):
    in_specs = (
        P(None, "gy", "gz", None),
        P(None, None, None, "gy", "gz", None),
        P(),
        P(),
        P(None, "gy", "gz", None),
    )
    out_specs = (
        P(None, "gy", "gz", None),
        P(None, "gy", "gz", None),
        P(None, None, None, "gy", "gz", None),
    )
    return jax.shard_map(shards, mesh=mesh, in_specs=in_specs, out_specs=out_specs, check_vma=False)
```

```python
import math

import numpy as np
import ml_dtypes

import jax
import jax.numpy as jnp
from jax import lax
from jax.experimental import pallas as pl
from jax.experimental.pallas import tpu as pltpu
from jax.sharding import PartitionSpec as P

C = 20
NX = 256
NY = 256
NZ = 128
MODES = 16
GY = 32
GZ = 8
YL = NY // GY
ZL = NZ // GZ
LANES = YL * ZL
TILES = 5
SEND_ROWS = TILES * 32
WEIGHT_ROWS = 56
GRAD_ROWS = 64
EXTRA = 748
COEF_ROWS = 768
KINDS = 40

f32 = jnp.float32
bf16 = jnp.bfloat16
VMEM_LIMIT = 8 * 1024 * 1024
WIDE_LIMIT = 20 * 1024 * 1024
DEEP_ROWS = 2 * 2 * LANES

GROUPS = (0, 160, 320, 480)


def halves(array):
    high = array.astype(np.float32).astype(ml_dtypes.bfloat16)
    low = (array - high.astype(np.float64)).astype(np.float32).astype(ml_dtypes.bfloat16)
    return high, low


def wide_table():
    x = np.arange(NX)
    freq = np.concatenate([np.arange(16), np.arange(1, 17), [16]])
    angle = 2.0 * math.pi * ((freq[:, None] * x[None, :]) % NX) / NX
    table = np.zeros((KINDS, NX))
    table[:33] = np.cos(angle)
    table[16:32] = -np.sin(angle[16:32])
    return table


def deep_table():
    z = np.arange(NZ)
    kz = np.arange(MODES)
    angle = 2.0 * math.pi * ((kz[:, None] * z[None, :]) % NZ) / NZ
    cos, sin = np.cos(angle), np.sin(angle)
    both = np.stack([np.stack([cos, -sin], 1), np.stack([sin, cos], 1)], 0)
    both = both.reshape(2, MODES, 2, GZ, ZL)
    table = np.einsum("akrgz,yv->gakryvz", both, np.eye(YL))
    return table.reshape(GZ, 2, 2 * MODES * YL, LANES)


def lat_table():
    row = np.arange(2 * MODES)
    ky = 4 * (row % 8) + row // 8
    fy = np.where(ky < MODES, ky, ky - 2 * MODES)
    y = np.arange(NY)
    angle = 2.0 * math.pi * ((fy[:, None] * y[None, :]) % NY) / NY
    return np.concatenate([np.cos(angle), np.sin(angle)], 0)


def split(value):
    high = value.astype(bf16)
    low = (value - high.astype(f32)).astype(bf16)
    return high, low


def dot(left, right, dims=((1,), (0,))):
    return lax.dot_general(left, right, (dims, ((), ())), preferred_element_type=f32)


def dot3(left, right, dims=((1,), (0,))):
    return (
        dot(left[0], right[0], dims) + dot(left[0], right[1], dims) + dot(left[1], right[0], dims)
    )


def lane_index(shape):
    return lax.broadcasted_iota(jnp.int32, shape, len(shape) - 1)


def turn(value, amount):
    amount = amount % 128
    return value if amount == 0 else pltpu.roll(value, amount, 1)


def times_i(value):
    lane = lane_index(value.shape) % 64
    turned = jnp.where(lane < C, -turn(value, -C), turn(value, C))
    return jnp.where(lane < 2 * C, turned, 0.0)


PAIR = 2


def wide_forward(tables, values, coef_ref, channel):
    part = dot(jnp.concatenate(split(values), 1), tables)
    for n in range(values.shape[0] // LANES):
        rows = part[LANES * n : LANES * n + LANES].T
        rows = rows[:KINDS] + rows[64 : 64 + KINDS]
        for k, start in enumerate(GROUPS):
            coef_ref[pl.ds(start + channel + n, 8, stride=C), :] = rows[8 * k : 8 * k + 8]
        coef_ref[pl.ds(EXTRA + channel + n, 1), :] = rows[32:33]


def wide_inverse(coef_ref, table, channel):
    rows = [coef_ref[pl.ds(start + channel, 8, stride=C), :] for start in GROUPS]
    rows.append(coef_ref[pl.ds(EXTRA + channel, 1), :])
    rows.append(jnp.zeros((7, LANES), f32))
    coef = jnp.concatenate(rows, 0)
    high = coef.astype(bf16).astype(f32)
    stacked = jnp.concatenate([high, high, coef - high, jnp.zeros((8, LANES), f32)], 0)
    return dot(stacked.T.astype(bf16), table)


def clear_extra(coef_ref):
    coef_ref[640:EXTRA, :] = jnp.zeros((EXTRA - 640, LANES), f32)


def deep_forward(deep_ref, coef_ref, out_ref):
    def product(at, rows):
        high, low = split(rows)
        table = deep_ref[2 * LANES * at : 2 * LANES * at + 2 * LANES, :]
        return dot(table, jnp.concatenate([high, high, low], 1), ((1,), (1,)))

    real = product(0, jnp.concatenate([coef_ref[0:384, :], coef_ref[640:COEF_ROWS, :]], 0))
    imag = product(1, coef_ref[256:640, :])
    left = lane_index((2 * LANES, 128)) < 64
    tiles = (
        real[:, :128],
        real[:, 128:256],
        jnp.where(left, real[:, 256:384], imag[:, :128]),
        imag[:, 128:256],
        imag[:, 256:] - real[:, 384:],
    )
    for t, deep in enumerate(tiles):
        for g in range(GZ):
            out_ref[g, 32 * t : 32 * t + 32, :] = deep[32 * g : 32 * g + 32]


def deep_inverse(deep_ref, block_ref, coef_ref):
    def product(at, rows):
        high, low = split(rows)
        table = deep_ref[2 * LANES * at : 2 * LANES * at + 2 * LANES, : 2 * LANES]
        wide = dot(high, table)
        return wide[:, :LANES] + wide[:, LANES:] + dot(low, table[:, :LANES])

    sections = []
    for t in range(TILES):
        tile = jnp.concatenate([block_ref[g, 32 * t : 32 * t + 32, :] for g in range(GZ)], 0)
        sections.append(tile.T)
    rows = jnp.concatenate(sections, 0)
    real = product(0, jnp.concatenate([rows[:320], -rows[512:]], 0))
    coef_ref[0:320, :] = real[:320]
    coef_ref[640:COEF_ROWS, :] = real[320:]
    coef_ref[320:640, :] = product(1, rows[320:])


STEP_C = 10
OUT_C = 2
OUT_Y = 1
STEPS = C // STEP_C


class Fetch:
    def __init__(self, sems):
        self.sems = sems
        self.count = 0

    def start(self, source, target):
        copy = pltpu.make_async_copy(source, target, self.sems.at[self.count])
        self.count += 1
        copy.start()
        return copy


def fetch_deep(fetch, deep_hbm, deep):
    return fetch.start(deep_hbm.at[lax.axis_index("gz")], deep)


def pack_weights(weights_ref, out_ref):
    units = []
    for c in range(C):
        for ky in range(4):
            for low in range(2):
                for part in range(2):
                    units.append(weights_ref[c, part * 4 + ky, pl.ds(low, GZ, stride=2), :])
    for row in range(WEIGHT_ROWS):
        pieces = units[6 * row : 6 * row + 6]
        used = C * len(pieces)
        pieces.append(jnp.zeros((GZ, 128 - used), f32))
        out_ref[:, SEND_ROWS + row, :] = jnp.concatenate(pieces, 1)


def first_kernel(
    deep_hbm, tables_hbm, values_hbm, weights_hbm, bypass_hbm, out_ref, deep, tables, ahead_ref,
    back_ref, values, weights, bypass, coef, sems
):
    fetch = Fetch(sems)
    bypass_copy = fetch.start(bypass_hbm, bypass)
    tables_copy = fetch.start(tables_hbm, tables)
    copies = []
    for k in range(STEPS):
        part = pl.ds(k * STEP_C, STEP_C)
        copies.append(fetch.start(values_hbm.at[part], values.at[part]))
    deep_copy = fetch_deep(fetch, deep_hbm, deep)
    weights_copy = fetch.start(weights_hbm, weights)
    clear_extra(coef)
    bypass_copy.wait()
    ahead_ref[...] = bypass_blocks(bypass[...], ((1,), (1,)))
    back_ref[...] = bypass_blocks(bypass[...], ((1,), (0,)))
    tables_copy.wait()
    for k in range(STEPS):
        copies[k].wait()
        for channel in range(k * STEP_C, k * STEP_C + STEP_C, PAIR):
            both = values[channel : channel + PAIR].reshape(PAIR * LANES, NX)
            wide_forward(tables[...], both, coef, channel)
    weights_copy.wait()
    pack_weights(weights, out_ref)
    deep_copy.wait()
    deep_forward(deep, coef, out_ref)


def anywhere():
    return pl.BlockSpec(memory_space=pl.ANY)


def vmem():
    return pl.BlockSpec(memory_space=pltpu.VMEM)


def params(limit=VMEM_LIMIT):
    return pltpu.CompilerParams(vmem_limit_bytes=limit)


def first_call(deep, tables, values, weights, bypass):
    shape = (GZ, SEND_ROWS + WEIGHT_ROWS, 128)
    operands = (deep, tables, values, weights, bypass)
    blocks = jax.ShapeDtypeStruct((8 * C, 24 * C), bf16)
    return pl.pallas_call(
        first_kernel,
        in_specs=[pl.BlockSpec(memory_space=pltpu.HBM)] * len(operands),
        out_specs=[vmem()] * 5,
        out_shape=[
            jax.ShapeDtypeStruct(shape, f32),
            jax.ShapeDtypeStruct(deep.shape[1:], bf16),
            jax.ShapeDtypeStruct(tables.shape, bf16),
            blocks,
            blocks,
        ],
        scratch_shapes=[
            pltpu.VMEM(values.shape, f32),
            pltpu.VMEM(weights.shape, f32),
            pltpu.VMEM(bypass.shape, f32),
            pltpu.VMEM((COEF_ROWS, LANES), f32),
            pltpu.SemaphoreType.DMA((STEPS + 4,)),
        ],
        compiler_params=params(WIDE_LIMIT),
    )(*(pltpu.with_memory_space_constraint(a, pltpu.HBM) for a in operands))


def join_kernel(block_ref, out_ref):
    tiles = []
    for t in range(TILES):
        rows = slice(32 * t, 32 * t + 32)
        total = block_ref[0, rows, :]
        for g in range(1, GZ):
            total = total + block_ref[g, rows, :]
        tiles.append(total)
    joined = jnp.concatenate(tiles, 1)
    gap = jnp.zeros((YL, 64 - 2 * C), f32)

    def arranged(at):
        cut = joined[:, C * at : C * at + C]
        return jnp.concatenate([cut[0:8], cut[8:16], gap, cut[16:24], cut[24:32], gap], 1)

    out_ref[0:8, :] = arranged(0)
    for f in range(1, 16):
        real = arranged(f)
        imag = arranged(15 + f)
        out_ref[8 * f : 8 * f + 8, :] = real + imag
        out_ref[8 * (32 - f) : 8 * (32 - f) + 8, :] = real - imag
    out_ref[128:136, :] = -arranged(31)


def join_call(block):
    return pl.pallas_call(
        join_kernel,
        in_specs=[vmem()],
        out_specs=vmem(),
        out_shape=jax.ShapeDtypeStruct((NY, 128), f32),
        compiler_params=params(),
    )(block)


def fork_blocks(block_ref, out_ref):
    blocks = [block_ref[0:8, :]]
    differences = []
    for f in range(1, 16):
        plus = block_ref[8 * f : 8 * f + 8, :]
        minus = block_ref[8 * (32 - f) : 8 * (32 - f) + 8, :]
        blocks.append(plus + minus)
        differences.append(plus - minus)
    blocks = blocks + differences + [-block_ref[128:136, :]]
    for k in range(4):
        lane = 64 * (k // 2) + C * (k % 2)
        row = jnp.concatenate([b[:, lane : lane + C] for b in blocks], 1)
        for t in range(TILES):
            out_ref[0, 32 * t + 8 * k : 32 * t + 8 * k + 8, :] = row[:, 128 * t : 128 * t + 128]


def fork_kernel(block_ref, out_ref):
    fork_blocks(block_ref, out_ref)


def fork_grads_kernel(block_ref, modes_ref, grad_ref, out_ref):
    fork_blocks(block_ref, out_ref)
    out_ref[0, SEND_ROWS : SEND_ROWS + 32, :] = modes_ref[...]
    out_ref[0, SEND_ROWS + 32 :, :] = grad_ref[...]


def fork_call(block, *grads):
    rows = SEND_ROWS + (GRAD_ROWS if grads else 0)
    return pl.pallas_call(
        fork_grads_kernel if grads else fork_kernel,
        in_specs=[vmem()] * (1 + len(grads)),
        out_specs=vmem(),
        out_shape=jax.ShapeDtypeStruct((1, rows, 128), f32),
        compiler_params=params(),
    )(block, *grads)


def unpack(block_ref, c):
    left = lane_index((GZ, 128)) < 64
    rows = []
    loaded = {}
    for ky in range(4):
        sides = []
        for low in range(2):
            unit = (c * 4 + ky) * 2 + low
            row = SEND_ROWS + unit // 3
            if row not in loaded:
                loaded[row] = block_ref[:, row, :]
            sides.append(turn(loaded[row], 64 * low - 40 * (unit % 3)))
        rows.append(jnp.where(left, sides[0], sides[1]))
    return jnp.concatenate(rows, 0)


def stacked(value):
    high, low = split(value)
    return jnp.concatenate([high, high, low], 0)


def lat_forward(lat_ref, block):
    both = dot(lat_ref[...], stacked(block))
    return both[:32] - times_i(both[32:])


def lat_inverse(back_ref, modes):
    return dot(back_ref[...], stacked(jnp.concatenate([modes, times_i(modes)], 0)))


def spread_table():
    table = np.zeros((128, C, 2, 128))
    for c in range(C):
        for part in range(2):
            for low in range(2):
                table[64 * low + C * part + c, c, part, 64 * low : 64 * low + 64] = 1
    return table.reshape(128, 2 * 128 * C)


SCALING = 1.0 / math.sqrt(NX * NY * NZ)


def depth_factor():
    lane = lane_index((32, 128))
    first = (lane < 64) & (lax.axis_index("gz") == 0)
    scale = 1.0 / (2.0 * math.sqrt(4.0 * MODES * MODES * MODES))
    factor = jnp.where(first, f32(scale), f32(2.0 * scale))
    return jnp.where(lane % 64 < 2 * C, factor, 0.0)


def mix_kernel(
    lat_ref, inverse_ref, spread_ref, block_ref, first_ref, out_ref, modes_ref, weights_ref
):
    modes = lat_forward(lat_ref, block_ref[...]) * SCALING
    modes_ref[...] = modes
    both = dot(jnp.concatenate(split(modes), 0), spread_ref[...])
    wide = both[:32] + both[32:]
    direct = jnp.zeros((32, 128), f32)
    crossed = jnp.zeros((32, 128), f32)
    for c in range(C):
        weight = unpack(first_ref, c)
        weights_ref[c] = weight
        at = 256 * c
        direct = direct + wide[:, at : at + 128] * weight
        crossed = crossed + wide[:, at + 128 : at + 256] * weight
    mixed = (direct + times_i(crossed)) * depth_factor()
    out_ref[...] = lat_inverse(inverse_ref, mixed)


def mix_call(lat, spreads, block, first):
    return pl.pallas_call(
        mix_kernel,
        in_specs=[vmem()] * 5,
        out_specs=[vmem()] * 3,
        out_shape=[
            jax.ShapeDtypeStruct((NY, 128), f32),
            jax.ShapeDtypeStruct((32, 128), f32),
            jax.ShapeDtypeStruct((C, 32, 128), f32),
        ],
        compiler_params=params(),
    )(*lat, spreads, block, first)


def join_table():
    table = np.zeros((C, 2, 128, 128))
    for c in range(C):
        for part in range(2):
            for low in range(2):
                table[c, part, 64 * low : 64 * low + 2 * C, 64 * low + C * part + c] = 1
    return table.reshape(2 * 128 * C, 128)


def adjoint_kernel(
    lat_ref, inverse_ref, join_ref, block_ref, weights_ref, out_ref, grad_ref
):
    grad = lat_forward(lat_ref, block_ref[...]) * depth_factor()
    grad_ref[...] = grad
    crossed = -times_i(grad)
    terms = []
    for c in range(C):
        weight = weights_ref[c]
        terms += [weight * grad, weight * crossed]
    high, low = split(jnp.concatenate(terms, 1))
    both = dot(jnp.concatenate([high, low], 0), join_ref[...])
    block = both[:32] + both[32:]
    out_ref[...] = lat_inverse(inverse_ref, block * SCALING)


def adjoint_call(lat, joins, block, weights):
    return pl.pallas_call(
        adjoint_kernel,
        in_specs=[vmem()] * 5,
        out_specs=[vmem()] * 2,
        out_shape=[
            jax.ShapeDtypeStruct((NY, 128), f32),
            jax.ShapeDtypeStruct((32, 128), f32),
        ],
        compiler_params=params(),
    )(*lat, joins, block, weights)


ROOT = math.sqrt(2.0 / math.pi)
CUBE = 0.044715


def bypass_blocks(bypass, dims):
    row = lax.broadcasted_iota(jnp.int32, (8 * C, C), 0)
    column = lax.broadcasted_iota(jnp.int32, (8 * C, C), 1)
    select = (row // 8 == column).astype(f32).astype(bf16)
    row = lax.broadcasted_iota(jnp.int32, (8 * C, 8 * C), 0)
    column = lax.broadcasted_iota(jnp.int32, (8 * C, 8 * C), 1)
    same = row % 8 == column % 8
    blocks = []
    for half in split(bypass):
        wide = dot(dot(select, half, dims).astype(bf16), select, ((1,), (1,)))
        blocks.append(jnp.where(same, wide, 0.0))
    return jnp.concatenate([blocks[0], blocks[1], blocks[0]], 1).astype(bf16)


def bypass_product(blocks, values):
    high, low = split(values)
    return dot(blocks, jnp.concatenate([high, high, low], 0))


def bypass_rows(blocks, values_ref, field):
    for y in range(YL):
        for half in range(2):
            rows = slice(8 * half, 8 * half + 8)
            place = slice(y * ZL + 8 * half, y * ZL + 8 * half + 8)
            values = values_ref[:, y, rows, :].reshape(8 * C, NX)
            field[:, place, :] = bypass_product(blocks, values).reshape(C, 8, NX)


def layer_kernel(
    back_ref, deep, tables_ref, bypass_ref, bias_hbm, block_ref, values_ref, cot_ref, out_hbm, slope_ref,
    send_ref, bias, field, outs, coef, coef_next, small_sems, sems
):
    fetch = Fetch(small_sems)
    bias_copy = fetch.start(bias_hbm, bias)

    def out_copy(part):
        group = pl.ds(part * OUT_C, OUT_C)
        return pltpu.make_async_copy(outs.at[group], out_hbm.at[group], sems.at[part])

    bypass_rows(bypass_ref[...], values_ref, field)
    deep_inverse(deep, block_ref, coef)
    bias_copy.wait()
    for step in range(C // PAIR):
        slopes = []
        for channel in range(PAIR * step, PAIR * step + PAIR):
            before = wide_inverse(coef, back_ref[...], channel) + field[channel] + bias[channel]
            square = before * before
            bend = jnp.tanh(before * (ROOT + (ROOT * CUBE) * square))
            half_up = 0.5 + 0.5 * bend
            rate = half_up + (half_up - half_up * half_up) * before * (
                2.0 * ROOT + (6.0 * ROOT * CUBE) * square
            )
            slope = cot_ref[channel].reshape(LANES, NX) * rate
            outs[channel] = (before * half_up).reshape(YL, ZL, NX)
            if channel % OUT_C == OUT_C - 1:
                out_copy(channel // OUT_C).start()
            slope_ref[channel] = slope.reshape(YL, ZL, NX)
            slopes.append(slope)
        wide_forward(tables_ref[...], jnp.concatenate(slopes, 0), coef_next, PAIR * step)
    clear_extra(coef_next)
    deep_forward(deep, coef_next, send_ref)
    for part in range(C // OUT_C):
        out_copy(part).wait()


def grid_shape():
    return jax.ShapeDtypeStruct((C, YL, ZL, NX), f32)


def grid_buffer():
    return pltpu.VMEM((C, YL, ZL, NX), f32)


def layer_call(back, deep, tables, bypass, bias, block, values, cotangent):
    return pl.pallas_call(
        layer_kernel,
        in_specs=[vmem()] * 4 + [anywhere()] + [vmem()] * 3,
        out_specs=[anywhere(), vmem(), vmem()],
        out_shape=[
            grid_shape(),
            grid_shape(),
            jax.ShapeDtypeStruct((GZ, SEND_ROWS, 128), f32),
        ],
        scratch_shapes=[
            pltpu.SMEM((C,), f32),
            pltpu.VMEM((C, LANES, NX), f32),
            grid_buffer(),
            pltpu.VMEM((COEF_ROWS, LANES), f32),
            pltpu.VMEM((COEF_ROWS, LANES), f32),
            pltpu.SemaphoreType.DMA((2,)),
            pltpu.SemaphoreType.DMA((C // OUT_C,)),
        ],
        compiler_params=params(WIDE_LIMIT),
    )(back, deep, tables, bypass, bias, block, values, cotangent)


def last_kernel(
    back_ref, deep, bypass_ref, block_ref, slope_ref, out_hbm, weight_hbm, field, outs, coef,
    weight, modes_rows, grad_rows, small_sems, sems
):
    fetch = Fetch(small_sems)

    def out_copy(part):
        rows = pl.ds(part * OUT_Y, OUT_Y)
        return pltpu.make_async_copy(outs.at[:, rows], out_hbm.at[:, rows], sems.at[part])

    for ky in range(4):
        for low in range(2):
            rows = pl.ds(low, GZ, stride=2)
            own = SEND_ROWS + 8 * ky + lax.axis_index("gz")
            modes_rows[rows, :] = turn(block_ref[:, pl.ds(own, 1), :].reshape(GZ, 128), 64 * low)
            own = own + 32
            grad_rows[rows, :] = turn(block_ref[:, pl.ds(own, 1), :].reshape(GZ, 128), 64 * low)
        modes = modes_rows[...]
        grad_real = grad_rows[...]
        grad_imag = turn(grad_real, -C)
        for channel in range(C):
            real = modes[:, channel : channel + 1]
            imag = modes[:, C + channel : C + channel + 1]
            weight[channel, ky] = (real * grad_real + imag * grad_imag)[:, :C]
            weight[channel, 4 + ky] = (real * grad_imag - imag * grad_real)[:, :C]
    weight_copy = fetch.start(weight, weight_hbm)
    deep_inverse(deep, block_ref, coef)
    for channel in range(C):
        field[channel] = wide_inverse(coef, back_ref[...], channel)
    blocks = bypass_ref[...]
    for y in range(YL):
        for half in range(2):
            rows = slice(8 * half, 8 * half + 8)
            place = slice(y * ZL + 8 * half, y * ZL + 8 * half + 8)
            slopes = slope_ref[:, y, rows, :].reshape(8 * C, NX)
            total = bypass_product(blocks, slopes) + field[:, place, :].reshape(8 * C, NX)
            outs[:, y, rows, :] = total.reshape(C, 8, NX)
        if y % OUT_Y == OUT_Y - 1:
            out_copy(y // OUT_Y).start()
    for part in range(YL // OUT_Y):
        out_copy(part).wait()
    weight_copy.wait()


def last_call(back, deep, bypass, block, slopes):
    weight_shape = (C, 8, MODES, C)
    return pl.pallas_call(
        last_kernel,
        in_specs=[vmem()] * 5,
        out_specs=[anywhere(), anywhere()],
        out_shape=[grid_shape(), jax.ShapeDtypeStruct(weight_shape, f32)],
        scratch_shapes=[
            pltpu.VMEM((C, LANES, NX), f32),
            grid_buffer(),
            pltpu.VMEM((COEF_ROWS, LANES), f32),
            pltpu.VMEM(weight_shape, f32),
            pltpu.VMEM((MODES, 128), f32),
            pltpu.VMEM((MODES, 128), f32),
            pltpu.SemaphoreType.DMA((1,)),
            pltpu.SemaphoreType.DMA((YL // OUT_Y,)),
        ],
        compiler_params=params(WIDE_LIMIT),
    )(back, deep, bypass, block, slopes)


def exchange(block, axis):
    return lax.all_to_all(block, axis, split_axis=0, concat_axis=0, tiled=True)


def gather(block):
    return lax.all_gather(block, "gz", axis=0, tiled=True)


def over_y(rows):
    return exchange(rows.reshape(GY, YL, 128), "gy").reshape(NY, 128)


def shards(grid_values, spectral_weights, bypass_weight, bias_vector, cotangent):
    wide_high, wide_low = halves(wide_table())
    nothing = np.zeros((8, NX), ml_dtypes.bfloat16)
    back = jnp.asarray(np.concatenate([wide_high, wide_low, wide_high, nothing], 0))
    deep_high, deep_low = halves(deep_table())
    deep = np.concatenate([deep_high, deep_low, deep_high], 3).reshape(GZ, DEEP_ROWS, 3 * LANES)
    tables = np.zeros((2 * NX, LANES), ml_dtypes.bfloat16)
    tables[:NX, :KINDS] = wide_high.T
    tables[:NX, 64 : 64 + KINDS] = wide_low.T
    tables[NX:, :KINDS] = wide_high.T
    deep = jnp.asarray(deep)
    tables = jnp.asarray(tables)
    joins = jnp.asarray(join_table().astype(ml_dtypes.bfloat16))
    lat_full = lat_table()
    lat = tuple(
        jnp.asarray(np.concatenate([high, low, high], 1))
        for high, low in (halves(lat_full), halves(lat_full.T.copy()))
    )
    spreads = jnp.asarray(spread_table().astype(ml_dtypes.bfloat16))

    weights = jnp.transpose(spectral_weights, (0, 2, 3, 4, 5, 1)).reshape(C, 8, MODES, C)
    values = grid_values.reshape(C, LANES, NX)

    sent, deep, tables, ahead, behind = first_call(
        deep, tables, values, weights, bypass_weight
    )
    first = exchange(sent, "gz")
    rows, modes, mixing = mix_call(lat, spreads, over_y(join_call(first)), first)
    got = gather(fork_call(over_y(rows)))
    output, slopes, sent = layer_call(
        back, deep, tables, ahead, bias_vector, got, grid_values, cotangent
    )

    got = exchange(sent, "gz")
    rows, grad = adjoint_call(lat, joins, over_y(join_call(got)), mixing)
    got = gather(fork_call(over_y(rows), modes, grad))
    grad_values, weight_grad = last_call(back, deep, behind, got, slopes)
    weight_grad = weight_grad.reshape(C, 2, 1, 4, MODES, C)
    return output, grad_values, jnp.transpose(weight_grad, (0, 5, 1, 2, 3, 4))


def solution(mesh):
    in_specs = (
        P(None, "gy", "gz", None),
        P(None, None, None, "gy", "gz", None),
        P(),
        P(),
        P(None, "gy", "gz", None),
    )
    out_specs = (
        P(None, "gy", "gz", None),
        P(None, "gy", "gz", None),
        P(None, None, None, "gy", "gz", None),
    )
    return jax.shard_map(shards, mesh=mesh, in_specs=in_specs, out_specs=out_specs, check_vma=False)
```

```python
import math

import numpy as np
import ml_dtypes

import jax
import jax.numpy as jnp
from jax import lax
from jax.experimental import pallas as pl
from jax.experimental.pallas import tpu as pltpu
from jax.sharding import PartitionSpec as P

C = 20
NX = 256
NY = 256
NZ = 128
MODES = 16
GY = 32
GZ = 8
YL = NY // GY
ZL = NZ // GZ
LANES = YL * ZL
TILES = 5
SEND_ROWS = TILES * 32
WEIGHT_ROWS = 56
GRAD_ROWS = 64
EXTRA = 748
COEF_ROWS = 768
KINDS = 40

f32 = jnp.float32
bf16 = jnp.bfloat16
VMEM_LIMIT = 8 * 1024 * 1024
WIDE_LIMIT = 20 * 1024 * 1024
DEEP_ROWS = 2 * 2 * LANES

GROUPS = (0, 160, 320, 480)


def halves(array):
    high = array.astype(np.float32).astype(ml_dtypes.bfloat16)
    low = (array - high.astype(np.float64)).astype(np.float32).astype(ml_dtypes.bfloat16)
    return high, low


def wide_table():
    x = np.arange(NX)
    freq = np.concatenate([np.arange(16), np.arange(1, 17), [16]])
    angle = 2.0 * math.pi * ((freq[:, None] * x[None, :]) % NX) / NX
    table = np.zeros((KINDS, NX))
    table[:33] = np.cos(angle)
    table[16:32] = -np.sin(angle[16:32])
    return table


def deep_table():
    z = np.arange(NZ)
    kz = np.arange(MODES)
    angle = 2.0 * math.pi * ((kz[:, None] * z[None, :]) % NZ) / NZ
    cos, sin = np.cos(angle), np.sin(angle)
    both = np.stack([np.stack([cos, -sin], 1), np.stack([sin, cos], 1)], 0)
    both = both.reshape(2, MODES, 2, GZ, ZL)
    table = np.einsum("akrgz,yv->gakryvz", both, np.eye(YL))
    return table.reshape(GZ, 2, 2 * MODES * YL, LANES)


def lat_table():
    row = np.arange(2 * MODES)
    ky = 4 * (row % 8) + row // 8
    fy = np.where(ky < MODES, ky, ky - 2 * MODES)
    y = np.arange(NY)
    angle = 2.0 * math.pi * ((fy[:, None] * y[None, :]) % NY) / NY
    return np.concatenate([np.cos(angle), np.sin(angle)], 0)


def split(value):
    high = value.astype(bf16)
    low = (value - high.astype(f32)).astype(bf16)
    return high, low


def dot(left, right, dims=((1,), (0,))):
    return lax.dot_general(left, right, (dims, ((), ())), preferred_element_type=f32)


def dot3(left, right, dims=((1,), (0,))):
    return (
        dot(left[0], right[0], dims) + dot(left[0], right[1], dims) + dot(left[1], right[0], dims)
    )


def lane_index(shape):
    return lax.broadcasted_iota(jnp.int32, shape, len(shape) - 1)


def turn(value, amount):
    amount = amount % 128
    return value if amount == 0 else pltpu.roll(value, amount, 1)


def times_i(value):
    lane = lane_index(value.shape) % 64
    turned = jnp.where(lane < C, -turn(value, -C), turn(value, C))
    return jnp.where(lane < 2 * C, turned, 0.0)


PAIR = 2


def wide_forward(tables, values, coef_ref, channel):
    part = dot(jnp.concatenate(split(values), 1), tables)
    for n in range(values.shape[0] // LANES):
        rows = part[LANES * n : LANES * n + LANES].T
        rows = rows[:KINDS] + rows[64 : 64 + KINDS]
        for k, start in enumerate(GROUPS):
            coef_ref[pl.ds(start + channel + n, 8, stride=C), :] = rows[8 * k : 8 * k + 8]
        coef_ref[pl.ds(EXTRA + channel + n, 1), :] = rows[32:33]


def wide_inverse(coef_ref, table, channel):
    rows = [coef_ref[pl.ds(start + channel, 8, stride=C), :] for start in GROUPS]
    rows.append(coef_ref[pl.ds(EXTRA + channel, 1), :])
    rows.append(jnp.zeros((7, LANES), f32))
    coef = jnp.concatenate(rows, 0)
    high = coef.astype(bf16).astype(f32)
    stacked = jnp.concatenate([high, high, coef - high, jnp.zeros((8, LANES), f32)], 0)
    return dot(stacked.T.astype(bf16), table)


def clear_extra(coef_ref):
    coef_ref[640:EXTRA, :] = jnp.zeros((EXTRA - 640, LANES), f32)


def deep_forward(deep_ref, coef_ref, out_ref):
    def product(at, rows):
        high, low = split(rows)
        table = deep_ref[2 * LANES * at : 2 * LANES * at + 2 * LANES, :]
        return dot(table, jnp.concatenate([high, high, low], 1), ((1,), (1,)))

    real = product(0, jnp.concatenate([coef_ref[0:384, :], coef_ref[640:COEF_ROWS, :]], 0))
    imag = product(1, coef_ref[256:640, :])
    left = lane_index((2 * LANES, 128)) < 64
    tiles = (
        real[:, :128],
        real[:, 128:256],
        jnp.where(left, real[:, 256:384], imag[:, :128]),
        imag[:, 128:256],
        imag[:, 256:] - real[:, 384:],
    )
    for t, deep in enumerate(tiles):
        for g in range(GZ):
            out_ref[g, 32 * t : 32 * t + 32, :] = deep[32 * g : 32 * g + 32]


def deep_inverse(deep_ref, block_ref, coef_ref):
    def product(at, rows):
        high, low = split(rows)
        table = deep_ref[2 * LANES * at : 2 * LANES * at + 2 * LANES, :]
        table = [table[:, LANES * k : LANES * k + LANES] for k in range(3)]
        return dot(jnp.concatenate([high, high, low], 1), jnp.concatenate(table, 0))

    sections = []
    for t in range(TILES):
        tile = jnp.concatenate([block_ref[g, 32 * t : 32 * t + 32, :] for g in range(GZ)], 0)
        sections.append(tile.T)
    rows = jnp.concatenate(sections, 0)
    real = product(0, jnp.concatenate([rows[:320], -rows[512:]], 0))
    coef_ref[0:320, :] = real[:320]
    coef_ref[640:COEF_ROWS, :] = real[320:]
    coef_ref[320:640, :] = product(1, rows[320:])


STEP_C = 10
OUT_C = 2
OUT_Y = 1
STEPS = C // STEP_C


class Fetch:
    def __init__(self, sems):
        self.sems = sems
        self.count = 0

    def start(self, source, target):
        copy = pltpu.make_async_copy(source, target, self.sems.at[self.count])
        self.count += 1
        copy.start()
        return copy


def fetch_deep(fetch, deep_hbm, deep):
    return fetch.start(deep_hbm.at[lax.axis_index("gz")], deep)


def pack_weights(weights_ref, out_ref):
    units = []
    for c in range(C):
        for ky in range(4):
            for low in range(2):
                for part in range(2):
                    units.append(weights_ref[c, part * 4 + ky, pl.ds(low, GZ, stride=2), :])
    for row in range(WEIGHT_ROWS):
        pieces = units[6 * row : 6 * row + 6]
        used = C * len(pieces)
        pieces.append(jnp.zeros((GZ, 128 - used), f32))
        out_ref[:, SEND_ROWS + row, :] = jnp.concatenate(pieces, 1)


def first_kernel(
    deep_hbm, tables_hbm, values_hbm, weights_hbm, bypass_hbm, out_ref, deep, tables, ahead_ref,
    back_ref, values, weights, bypass, coef, sems
):
    fetch = Fetch(sems)
    bypass_copy = fetch.start(bypass_hbm, bypass)
    tables_copy = fetch.start(tables_hbm, tables)
    copies = []
    for k in range(STEPS):
        part = pl.ds(k * STEP_C, STEP_C)
        copies.append(fetch.start(values_hbm.at[part], values.at[part]))
    deep_copy = fetch_deep(fetch, deep_hbm, deep)
    weights_copy = fetch.start(weights_hbm, weights)
    clear_extra(coef)
    bypass_copy.wait()
    ahead_ref[...] = bypass_blocks(bypass[...], ((1,), (1,)))
    back_ref[...] = bypass_blocks(bypass[...], ((1,), (0,)))
    tables_copy.wait()
    for k in range(STEPS):
        copies[k].wait()
        for channel in range(k * STEP_C, k * STEP_C + STEP_C, PAIR):
            both = values[channel : channel + PAIR].reshape(PAIR * LANES, NX)
            wide_forward(tables[...], both, coef, channel)
    weights_copy.wait()
    pack_weights(weights, out_ref)
    deep_copy.wait()
    deep_forward(deep, coef, out_ref)


def anywhere():
    return pl.BlockSpec(memory_space=pl.ANY)


def vmem():
    return pl.BlockSpec(memory_space=pltpu.VMEM)


def params(limit=VMEM_LIMIT):
    return pltpu.CompilerParams(vmem_limit_bytes=limit)


def first_call(deep, tables, values, weights, bypass):
    shape = (GZ, SEND_ROWS + WEIGHT_ROWS, 128)
    operands = (deep, tables, values, weights, bypass)
    blocks = jax.ShapeDtypeStruct((8 * C, 24 * C), bf16)
    return pl.pallas_call(
        first_kernel,
        in_specs=[pl.BlockSpec(memory_space=pltpu.HBM)] * len(operands),
        out_specs=[vmem()] * 5,
        out_shape=[
            jax.ShapeDtypeStruct(shape, f32),
            jax.ShapeDtypeStruct(deep.shape[1:], bf16),
            jax.ShapeDtypeStruct(tables.shape, bf16),
            blocks,
            blocks,
        ],
        scratch_shapes=[
            pltpu.VMEM(values.shape, f32),
            pltpu.VMEM(weights.shape, f32),
            pltpu.VMEM(bypass.shape, f32),
            pltpu.VMEM((COEF_ROWS, LANES), f32),
            pltpu.SemaphoreType.DMA((STEPS + 4,)),
        ],
        compiler_params=params(WIDE_LIMIT),
    )(*(pltpu.with_memory_space_constraint(a, pltpu.HBM) for a in operands))


def join_kernel(block_ref, out_ref):
    tiles = []
    for t in range(TILES):
        rows = slice(32 * t, 32 * t + 32)
        total = block_ref[0, rows, :]
        for g in range(1, GZ):
            total = total + block_ref[g, rows, :]
        tiles.append(total)
    joined = jnp.concatenate(tiles, 1)
    gap = jnp.zeros((YL, 64 - 2 * C), f32)

    def arranged(at):
        cut = joined[:, C * at : C * at + C]
        return jnp.concatenate([cut[0:8], cut[8:16], gap, cut[16:24], cut[24:32], gap], 1)

    out_ref[0:8, :] = arranged(0)
    for f in range(1, 16):
        real = arranged(f)
        imag = arranged(15 + f)
        out_ref[8 * f : 8 * f + 8, :] = real + imag
        out_ref[8 * (32 - f) : 8 * (32 - f) + 8, :] = real - imag
    out_ref[128:136, :] = -arranged(31)


def join_call(block):
    return pl.pallas_call(
        join_kernel,
        in_specs=[vmem()],
        out_specs=vmem(),
        out_shape=jax.ShapeDtypeStruct((NY, 128), f32),
        compiler_params=params(),
    )(block)


def fork_blocks(block_ref, out_ref):
    blocks = [block_ref[0:8, :]]
    differences = []
    for f in range(1, 16):
        plus = block_ref[8 * f : 8 * f + 8, :]
        minus = block_ref[8 * (32 - f) : 8 * (32 - f) + 8, :]
        blocks.append(plus + minus)
        differences.append(plus - minus)
    blocks = blocks + differences + [-block_ref[128:136, :]]
    for k in range(4):
        lane = 64 * (k // 2) + C * (k % 2)
        row = jnp.concatenate([b[:, lane : lane + C] for b in blocks], 1)
        for t in range(TILES):
            out_ref[0, 32 * t + 8 * k : 32 * t + 8 * k + 8, :] = row[:, 128 * t : 128 * t + 128]


def fork_kernel(block_ref, out_ref):
    fork_blocks(block_ref, out_ref)


def fork_grads_kernel(block_ref, modes_ref, grad_ref, out_ref):
    fork_blocks(block_ref, out_ref)
    out_ref[0, SEND_ROWS : SEND_ROWS + 32, :] = modes_ref[...]
    out_ref[0, SEND_ROWS + 32 :, :] = grad_ref[...]


def fork_call(block, *grads):
    rows = SEND_ROWS + (GRAD_ROWS if grads else 0)
    return pl.pallas_call(
        fork_grads_kernel if grads else fork_kernel,
        in_specs=[vmem()] * (1 + len(grads)),
        out_specs=vmem(),
        out_shape=jax.ShapeDtypeStruct((1, rows, 128), f32),
        compiler_params=params(),
    )(block, *grads)


def unpack(block_ref, c):
    left = lane_index((GZ, 128)) < 64
    rows = []
    loaded = {}
    for ky in range(4):
        sides = []
        for low in range(2):
            unit = (c * 4 + ky) * 2 + low
            row = SEND_ROWS + unit // 3
            if row not in loaded:
                loaded[row] = block_ref[:, row, :]
            sides.append(turn(loaded[row], 64 * low - 40 * (unit % 3)))
        rows.append(jnp.where(left, sides[0], sides[1]))
    return jnp.concatenate(rows, 0)


def stacked(value):
    high, low = split(value)
    return jnp.concatenate([high, high, low], 0)


def lat_forward(lat_ref, block):
    both = dot(lat_ref[...], stacked(block))
    return both[:32] - times_i(both[32:])


def lat_inverse(back_ref, modes):
    return dot(back_ref[...], stacked(jnp.concatenate([modes, times_i(modes)], 0)))


def spread_table():
    table = np.zeros((128, C, 2, 128))
    for c in range(C):
        for part in range(2):
            for low in range(2):
                table[64 * low + C * part + c, c, part, 64 * low : 64 * low + 64] = 1
    return table.reshape(128, 2 * 128 * C)


SCALING = 1.0 / math.sqrt(NX * NY * NZ)


def depth_factor():
    lane = lane_index((32, 128))
    first = (lane < 64) & (lax.axis_index("gz") == 0)
    scale = 1.0 / (2.0 * math.sqrt(4.0 * MODES * MODES * MODES))
    factor = jnp.where(first, f32(scale), f32(2.0 * scale))
    return jnp.where(lane % 64 < 2 * C, factor, 0.0)


def mix_kernel(
    lat_ref, inverse_ref, spread_ref, block_ref, first_ref, out_ref, modes_ref, weights_ref
):
    modes = lat_forward(lat_ref, block_ref[...]) * SCALING
    modes_ref[...] = modes
    both = dot(jnp.concatenate(split(modes), 0), spread_ref[...])
    wide = both[:32] + both[32:]
    direct = jnp.zeros((32, 128), f32)
    crossed = jnp.zeros((32, 128), f32)
    for c in range(C):
        weight = unpack(first_ref, c)
        weights_ref[c] = weight
        at = 256 * c
        direct = direct + wide[:, at : at + 128] * weight
        crossed = crossed + wide[:, at + 128 : at + 256] * weight
    mixed = (direct + times_i(crossed)) * depth_factor()
    out_ref[...] = lat_inverse(inverse_ref, mixed)


def mix_call(lat, spreads, block, first):
    return pl.pallas_call(
        mix_kernel,
        in_specs=[vmem()] * 5,
        out_specs=[vmem()] * 3,
        out_shape=[
            jax.ShapeDtypeStruct((NY, 128), f32),
            jax.ShapeDtypeStruct((32, 128), f32),
            jax.ShapeDtypeStruct((C, 32, 128), f32),
        ],
        compiler_params=params(),
    )(*lat, spreads, block, first)


def join_table():
    table = np.zeros((C, 2, 128, 128))
    for c in range(C):
        for part in range(2):
            for low in range(2):
                table[c, part, 64 * low : 64 * low + 2 * C, 64 * low + C * part + c] = 1
    return table.reshape(2 * 128 * C, 128)


def adjoint_kernel(
    lat_ref, inverse_ref, join_ref, block_ref, weights_ref, out_ref, grad_ref
):
    grad = lat_forward(lat_ref, block_ref[...]) * depth_factor()
    grad_ref[...] = grad
    crossed = -times_i(grad)
    terms = []
    for c in range(C):
        weight = weights_ref[c]
        terms += [weight * grad, weight * crossed]
    high, low = split(jnp.concatenate(terms, 1))
    both = dot(jnp.concatenate([high, low], 0), join_ref[...])
    block = both[:32] + both[32:]
    out_ref[...] = lat_inverse(inverse_ref, block * SCALING)


def adjoint_call(lat, joins, block, weights):
    return pl.pallas_call(
        adjoint_kernel,
        in_specs=[vmem()] * 5,
        out_specs=[vmem()] * 2,
        out_shape=[
            jax.ShapeDtypeStruct((NY, 128), f32),
            jax.ShapeDtypeStruct((32, 128), f32),
        ],
        compiler_params=params(),
    )(*lat, joins, block, weights)


ROOT = math.sqrt(2.0 / math.pi)
CUBE = 0.044715


def bypass_blocks(bypass, dims):
    row = lax.broadcasted_iota(jnp.int32, (8 * C, C), 0)
    column = lax.broadcasted_iota(jnp.int32, (8 * C, C), 1)
    select = (row // 8 == column).astype(f32).astype(bf16)
    row = lax.broadcasted_iota(jnp.int32, (8 * C, 8 * C), 0)
    column = lax.broadcasted_iota(jnp.int32, (8 * C, 8 * C), 1)
    same = row % 8 == column % 8
    blocks = []
    for half in split(bypass):
        wide = dot(dot(select, half, dims).astype(bf16), select, ((1,), (1,)))
        blocks.append(jnp.where(same, wide, 0.0))
    return jnp.concatenate([blocks[0], blocks[1], blocks[0]], 1).astype(bf16)


def bypass_product(blocks, values):
    high, low = split(values)
    return dot(blocks, jnp.concatenate([high, high, low], 0))


def bypass_rows(blocks, values_ref, field):
    for y in range(YL):
        for half in range(2):
            rows = slice(8 * half, 8 * half + 8)
            place = slice(y * ZL + 8 * half, y * ZL + 8 * half + 8)
            values = values_ref[:, y, rows, :].reshape(8 * C, NX)
            field[:, place, :] = bypass_product(blocks, values).reshape(C, 8, NX)


def layer_kernel(
    back_ref, deep, tables_ref, bypass_ref, bias_hbm, block_ref, values_ref, cot_ref, out_hbm, slope_ref,
    send_ref, bias, field, outs, coef, coef_next, small_sems, sems
):
    fetch = Fetch(small_sems)
    bias_copy = fetch.start(bias_hbm, bias)

    def out_copy(part):
        group = pl.ds(part * OUT_C, OUT_C)
        return pltpu.make_async_copy(outs.at[group], out_hbm.at[group], sems.at[part])

    bypass_rows(bypass_ref[...], values_ref, field)
    deep_inverse(deep, block_ref, coef)
    bias_copy.wait()
    for step in range(C // PAIR):
        slopes = []
        for channel in range(PAIR * step, PAIR * step + PAIR):
            before = wide_inverse(coef, back_ref[...], channel) + field[channel] + bias[channel]
            square = before * before
            bend = jnp.tanh(before * (ROOT + (ROOT * CUBE) * square))
            half_up = 0.5 + 0.5 * bend
            rate = half_up + (half_up - half_up * half_up) * before * (
                2.0 * ROOT + (6.0 * ROOT * CUBE) * square
            )
            slope = cot_ref[channel].reshape(LANES, NX) * rate
            outs[channel] = (before * half_up).reshape(YL, ZL, NX)
            if channel % OUT_C == OUT_C - 1:
                out_copy(channel // OUT_C).start()
            slope_ref[channel] = slope.reshape(YL, ZL, NX)
            slopes.append(slope)
        wide_forward(tables_ref[...], jnp.concatenate(slopes, 0), coef_next, PAIR * step)
    clear_extra(coef_next)
    deep_forward(deep, coef_next, send_ref)
    for part in range(C // OUT_C):
        out_copy(part).wait()


def grid_shape():
    return jax.ShapeDtypeStruct((C, YL, ZL, NX), f32)


def grid_buffer():
    return pltpu.VMEM((C, YL, ZL, NX), f32)


def layer_call(back, deep, tables, bypass, bias, block, values, cotangent):
    return pl.pallas_call(
        layer_kernel,
        in_specs=[vmem()] * 4 + [anywhere()] + [vmem()] * 3,
        out_specs=[anywhere(), vmem(), vmem()],
        out_shape=[
            grid_shape(),
            grid_shape(),
            jax.ShapeDtypeStruct((GZ, SEND_ROWS, 128), f32),
        ],
        scratch_shapes=[
            pltpu.SMEM((C,), f32),
            pltpu.VMEM((C, LANES, NX), f32),
            grid_buffer(),
            pltpu.VMEM((COEF_ROWS, LANES), f32),
            pltpu.VMEM((COEF_ROWS, LANES), f32),
            pltpu.SemaphoreType.DMA((2,)),
            pltpu.SemaphoreType.DMA((C // OUT_C,)),
        ],
        compiler_params=params(WIDE_LIMIT),
    )(back, deep, tables, bypass, bias, block, values, cotangent)


def last_kernel(
    back_ref, deep, bypass_ref, block_ref, slope_ref, out_hbm, weight_hbm, field, outs, coef,
    weight, modes_rows, grad_rows, small_sems, sems
):
    fetch = Fetch(small_sems)

    def out_copy(part):
        rows = pl.ds(part * OUT_Y, OUT_Y)
        return pltpu.make_async_copy(outs.at[:, rows], out_hbm.at[:, rows], sems.at[part])

    for ky in range(4):
        for low in range(2):
            rows = pl.ds(low, GZ, stride=2)
            own = SEND_ROWS + 8 * ky + lax.axis_index("gz")
            modes_rows[rows, :] = turn(block_ref[:, pl.ds(own, 1), :].reshape(GZ, 128), 64 * low)
            own = own + 32
            grad_rows[rows, :] = turn(block_ref[:, pl.ds(own, 1), :].reshape(GZ, 128), 64 * low)
        modes = modes_rows[...]
        grad_real = grad_rows[...]
        grad_imag = turn(grad_real, -C)
        for channel in range(C):
            real = modes[:, channel : channel + 1]
            imag = modes[:, C + channel : C + channel + 1]
            weight[channel, ky] = (real * grad_real + imag * grad_imag)[:, :C]
            weight[channel, 4 + ky] = (real * grad_imag - imag * grad_real)[:, :C]
    weight_copy = fetch.start(weight, weight_hbm)
    deep_inverse(deep, block_ref, coef)
    for channel in range(C):
        field[channel] = wide_inverse(coef, back_ref[...], channel)
    blocks = bypass_ref[...]
    for y in range(YL):
        for half in range(2):
            rows = slice(8 * half, 8 * half + 8)
            place = slice(y * ZL + 8 * half, y * ZL + 8 * half + 8)
            slopes = slope_ref[:, y, rows, :].reshape(8 * C, NX)
            total = bypass_product(blocks, slopes) + field[:, place, :].reshape(8 * C, NX)
            outs[:, y, rows, :] = total.reshape(C, 8, NX)
        if y % OUT_Y == OUT_Y - 1:
            out_copy(y // OUT_Y).start()
    for part in range(YL // OUT_Y):
        out_copy(part).wait()
    weight_copy.wait()


def last_call(back, deep, bypass, block, slopes):
    weight_shape = (C, 8, MODES, C)
    return pl.pallas_call(
        last_kernel,
        in_specs=[vmem()] * 5,
        out_specs=[anywhere(), anywhere()],
        out_shape=[grid_shape(), jax.ShapeDtypeStruct(weight_shape, f32)],
        scratch_shapes=[
            pltpu.VMEM((C, LANES, NX), f32),
            grid_buffer(),
            pltpu.VMEM((COEF_ROWS, LANES), f32),
            pltpu.VMEM(weight_shape, f32),
            pltpu.VMEM((MODES, 128), f32),
            pltpu.VMEM((MODES, 128), f32),
            pltpu.SemaphoreType.DMA((1,)),
            pltpu.SemaphoreType.DMA((YL // OUT_Y,)),
        ],
        compiler_params=params(WIDE_LIMIT),
    )(back, deep, bypass, block, slopes)


def exchange(block, axis):
    return lax.all_to_all(block, axis, split_axis=0, concat_axis=0, tiled=True)


def gather(block):
    return lax.all_gather(block, "gz", axis=0, tiled=True)


def over_y(rows):
    return exchange(rows.reshape(GY, YL, 128), "gy").reshape(NY, 128)


def shards(grid_values, spectral_weights, bypass_weight, bias_vector, cotangent):
    wide_high, wide_low = halves(wide_table())
    nothing = np.zeros((8, NX), ml_dtypes.bfloat16)
    back = jnp.asarray(np.concatenate([wide_high, wide_low, wide_high, nothing], 0))
    deep_high, deep_low = halves(deep_table())
    deep = np.concatenate([deep_high, deep_low, deep_high], 3).reshape(GZ, DEEP_ROWS, 3 * LANES)
    tables = np.zeros((2 * NX, LANES), ml_dtypes.bfloat16)
    tables[:NX, :KINDS] = wide_high.T
    tables[:NX, 64 : 64 + KINDS] = wide_low.T
    tables[NX:, :KINDS] = wide_high.T
    deep = jnp.asarray(deep)
    tables = jnp.asarray(tables)
    joins = jnp.asarray(join_table().astype(ml_dtypes.bfloat16))
    lat_full = lat_table()
    lat = tuple(
        jnp.asarray(np.concatenate([high, low, high], 1))
        for high, low in (halves(lat_full), halves(lat_full.T.copy()))
    )
    spreads = jnp.asarray(spread_table().astype(ml_dtypes.bfloat16))

    weights = jnp.transpose(spectral_weights, (0, 2, 3, 4, 5, 1)).reshape(C, 8, MODES, C)
    values = grid_values.reshape(C, LANES, NX)

    sent, deep, tables, ahead, behind = first_call(
        deep, tables, values, weights, bypass_weight
    )
    first = exchange(sent, "gz")
    rows, modes, mixing = mix_call(lat, spreads, over_y(join_call(first)), first)
    got = gather(fork_call(over_y(rows)))
    output, slopes, sent = layer_call(
        back, deep, tables, ahead, bias_vector, got, grid_values, cotangent
    )

    got = exchange(sent, "gz")
    rows, grad = adjoint_call(lat, joins, over_y(join_call(got)), mixing)
    got = gather(fork_call(over_y(rows), modes, grad))
    grad_values, weight_grad = last_call(back, deep, behind, got, slopes)
    weight_grad = weight_grad.reshape(C, 2, 1, 4, MODES, C)
    return output, grad_values, jnp.transpose(weight_grad, (0, 5, 1, 2, 3, 4))


def solution(mesh):
    in_specs = (
        P(None, "gy", "gz", None),
        P(None, None, None, "gy", "gz", None),
        P(),
        P(),
        P(None, "gy", "gz", None),
    )
    out_specs = (
        P(None, "gy", "gz", None),
        P(None, "gy", "gz", None),
        P(None, None, None, "gy", "gz", None),
    )
    return jax.shard_map(shards, mesh=mesh, in_specs=in_specs, out_specs=out_specs, check_vma=False)
```
